512 devices in a mesh: space: 32 (over y_hi, x, core), chan: 16 (over y_lo, z).
Axes of the slice: x: 4, y: 8 (y_hi: 4, y_lo: 2; y = y_hi * 2 + y_lo), z: 8, core: 2. Of those that a mesh axis runs over, the one named last changes fastest.
Arguments:
- field: bfloat16 [256, 64, 4, 128], P('chan', 'space'), may hold values from -6 to 6
- filters: bfloat16 [27, 256, 256], P(None, 'chan'), may hold values from -0.078125 to 0.078125
- cotangent: bfloat16 [256, 64, 4, 128], P('chan', 'space'), may hold values from -6 to 6
Outputs:
- out_field: bfloat16 [256, 64, 4, 128], P('chan', 'space')
- input_grad: bfloat16 [256, 64, 4, 128], P('chan', 'space')
- weight_grad: float32 [27, 256, 256], P(None, 'chan')
The draws below stay inside these ranges and needn't reach their ends.
All inputs are finite; a program needn't handle non-finite values.
Results may differ from the reference program's by a relative error of at most 0.001.
Values may be sent and summed in bfloat16 or wider, within the bound.
No kernel may reach another device: no remote copies, remote signals or barrier semaphores. Data moves between devices by JAX's collectives and lax.ppermute only.
A program may use at most 128 MiB of HBM per device.

```python
import math
import jax
import jax.numpy as jnp
from jax import lax

C = 256
PLANES = 4
YC = 128
NX = 64


def block_scale(own_key, shape, split, low, top_value):
    def one(position, shards_of):
        steps = jax.random.uniform(jax.random.fold_in(jax.random.fold_in(own_key, 6), position), (shards_of,), jnp.float32, low / len(split), top_value / len(split))
        return jnp.repeat(jnp.exp(steps), shape[position] // shards_of).reshape((-1,) + (1,) * (len(shape) - position - 1))

    gain = one(*split[0])
    for cut in split[1:]:
        gain = gain * one(*cut)
    return gain


def bell_draw(rng, dims, width, most, cuts=(), held_as=jnp.bfloat16):
    array = jax.random.normal(rng, dims, jnp.float32) * width
    if len(cuts) > 0:
        array = block_scale(rng, dims, cuts, -0.22, 0.18) * array
    return jnp.clip(array, min=-most, max=most).astype(held_as)


def setup_inputs(seed: int = 0) -> dict:
    streams_of = jax.random.split(jax.random.key(seed), 4)
    field = bell_draw(streams_of[0], (C, NX, PLANES, YC), 1.0, 6.0, ((0, 16), (1, 32)))
    filters = bell_draw(streams_of[1], (27, C, C), (27 * C) ** -0.5, 0.078125, ((1, 16),))
    cotangent = bell_draw(streams_of[2], (C, NX, PLANES, YC), 1.0, 6.0, ((0, 16), (1, 32)))
    return dict(field=field, filters=filters, cotangent=cotangent)


def reference(field, filters, cotangent):
    cell_count = NX * PLANES * YC
    pads = ((0, 0), (2, 2), (2, 2), (2, 2))
    padded_field = jnp.pad(field, pads)
    padded_cot = jnp.pad(cotangent, pads)
    flat_cot = cotangent.reshape(C, cell_count)
    forward_sum = jnp.zeros((C, cell_count), jnp.float32)
    adjoint_sum = jnp.zeros((C, cell_count), jnp.float32)
    blocks = []
    for k in range(27):
        a, b, c = (k // 9, k // 3 % 3, k % 3)
        window = padded_field[:, 2 * a:2 * a + NX, 2 * b:2 * b + PLANES, 2 * c:2 * c + YC].reshape(C, cell_count)
        forward_sum = forward_sum + jnp.dot(filters[k], window, preferred_element_type=jnp.float32)
        blocks.append(lax.dot_general(flat_cot, window, (((1,), (1,)), ((), ())), preferred_element_type=jnp.float32))
        back_window = padded_cot[:, 4 - 2 * a:4 - 2 * a + NX, 4 - 2 * b:4 - 2 * b + PLANES, 4 - 2 * c:4 - 2 * c + YC].reshape(C, cell_count)
        adjoint_sum = adjoint_sum + lax.dot_general(filters[k], back_window, (((0,), (0,)), ((), ())), preferred_element_type=jnp.float32)
    scale = 1.0 / math.sqrt(NX * PLANES * YC)
    out_field = forward_sum.astype(jnp.bfloat16).reshape(C, NX, PLANES, YC)
    input_grad = adjoint_sum.astype(jnp.bfloat16).reshape(C, NX, PLANES, YC)
    weight_grad = jnp.stack(blocks) * scale
    return (out_field, input_grad, weight_grad)
```

```python
import functools
import math

import jax
import jax.numpy as jnp
from jax import lax
from jax.experimental import pallas as pl
from jax.experimental.pallas import tpu as pltpu
from jax.sharding import Mesh
from jax.sharding import PartitionSpec as P

BF = jnp.bfloat16
F32 = jnp.float32
VMEM = pl.BlockSpec(memory_space=pltpu.VMEM)
SMEM = pl.BlockSpec(memory_space=pltpu.SMEM)
TAPS = 27
OWN = 16
CELLS = 1024
ROWS = TAPS * OWN
WIDE = CELLS + 512
LIMIT = 48 * 1024 * 1024


def call(body, outs, ins, scratch=(), flops=0, moved=0):
    return pl.pallas_call(
        body,
        out_shape=outs,
        in_specs=ins,
        out_specs=[VMEM] * len(outs),
        scratch_shapes=list(scratch),
        compiler_params=pltpu.CompilerParams(vmem_limit_bytes=LIMIT),
        cost_estimate=pl.CostEstimate(flops=flops, bytes_accessed=moved, transcendentals=0),
    )


def shape(dims, kind):
    return jax.ShapeDtypeStruct(dims, kind)


def lanes(dims):
    return lax.broadcasted_iota(jnp.int32, dims, len(dims) - 1)


def moved_by(block, step):
    if step == 0:
        return block
    at = lanes(block.shape) + step
    turned = pltpu.roll(block, (-step) % 128, 1)
    return jnp.where((at >= 0) & (at < 128), turned, 0.0)


def pack_body(field, filters, out):
    own = field[...]
    for c in range(16):
        out[c, :, 0:CELLS] = own
    lane = lanes((OWN, 128))
    for g in range(4):
        parts = [jnp.zeros((OWN, 128), F32) for _ in range(16)]
        for j in range(8):
            k = 8 * g + j
            if k >= TAPS:
                break
            here = (lane >= 16 * j) & (lane < 16 * j + 16)
            for h in range(2):
                block = filters[k, :, 128 * h : 128 * h + 128].astype(F32)
                for q in range(8):
                    step = (16 * (j - q)) % 128
                    turned = block if step == 0 else pltpu.roll(block, step, 1)
                    parts[8 * h + q] = jnp.where(here, turned, parts[8 * h + q])
        for c in range(16):
            out[c, :, CELLS + 128 * g : CELLS + 128 * g + 128] = parts[c].astype(BF)


def taps_sum(products, a, sign):
    blocks = []
    for r in range(2):
        for z in range(4):
            total = None
            for c in range(3):
                column = None
                for b in range(3):
                    source = z + sign * 2 * (b - 1)
                    if source < 0 or source > 3:
                        continue
                    k = 9 * a + 3 * b + c
                    lane = 128 * (4 * r + source)
                    part = products[16 * k : 16 * k + 16, lane : lane + 128]
                    column = part if column is None else column + part
                column = moved_by(column, sign * 2 * (c - 1))
                total = column if total is None else total + column
            blocks.append(total)
    return blocks


def grad_body(core, gathered, below, own, above, keep, send, shifted):
    zero = jnp.zeros((OWN, 128), BF)
    for a, source in ((0, above), (1, own), (2, below)):
        for r in range(2):
            rolled = []
            for z in range(4):
                lane = 128 * (4 * r + z)
                block = source[:, lane : lane + 128].astype(F32)
                rolled.append([moved_by(block, -2 * (c - 1)).astype(BF) for c in range(3)])
            for z in range(4):
                for b in range(3):
                    at = z - 2 * (b - 1)
                    for c in range(3):
                        k = 9 * a + 3 * b + c
                        lane = 128 * (4 * r + z)
                        shifted[16 * k : 16 * k + 16, lane : lane + 128] = (
                            rolled[at][c] if 0 <= at < 4 else zero
                        )
    total = lax.dot_general(
        shifted[...],
        gathered[:, 0:CELLS],
        (((1,), (1,)), ((), ())),
        preferred_element_type=F32,
    )
    low, high = total[:, 0:128], total[:, 128:256]
    first = core[0] == 0
    keep[0:ROWS, :] = jnp.where(first, low, high)
    keep[ROWS:512, :] = jnp.zeros((512 - ROWS, 128), F32)
    send[...] = jnp.where(first, high, low)


def forward_body(gathered, filters, out, products):
    products[...] = jnp.dot(
        filters[...].reshape(ROWS, 256), gathered[:, 0:CELLS], preferred_element_type=F32
    )
    for a in range(3):
        for n, block in enumerate(taps_sum(products, a, 1)):
            out[a, :, 128 * n : 128 * n + 128] = block


def adjoint_body(gathered, cotangent, out, products):
    products[...] = lax.dot_general(
        gathered[:, CELLS : CELLS + ROWS],
        cotangent[...],
        (((0,), (0,)), ((), ())),
        preferred_element_type=F32,
    )
    for a in range(3):
        for n, block in enumerate(taps_sum(products, a, -1)):
            out[a, :, 128 * n : 128 * n + 128] = block


def per_device(field, filters, cotangent):
    scale = 1.0 / math.sqrt(32768)
    space = ("pair", "core")
    core = lax.axis_index("core").astype(jnp.int32).reshape(1)
    own_field = field.reshape(OWN, CELLS)
    own_cot = cotangent.reshape(OWN, CELLS)

    up = [(i, i + 1) for i in range(31)]
    down = [(i + 1, i) for i in range(31)]
    below = lax.ppermute(own_cot, space, up)
    above = lax.ppermute(own_cot, space, down)
    wide_cot = jnp.concatenate([own_cot, jnp.zeros_like(own_cot)], axis=0)
    all_cot = lax.all_gather(wide_cot, "chan", axis=0, tiled=False)[:, :OWN].reshape(256, CELLS)

    packed = call(pack_body, [shape((16, OWN, WIDE), BF)], [VMEM] * 2, moved=1 << 20)(
        own_field, filters
    )[0]
    gathered = lax.all_to_all(packed, "chan", 0, 0).reshape(256, WIDE)

    keep, send = call(
        grad_body,
        [shape((512, 128), F32), shape((ROWS, 128), F32)],
        [SMEM] + [VMEM] * 4,
        [pltpu.VMEM((ROWS, CELLS), BF)],
        flops=2 * ROWS * CELLS * 256,
        moved=1 << 20,
    )(core, gathered, below, own_cot, above)
    swapped = lax.ppermute(send, "core", [(0, 1), (1, 0)])
    ys = call(
        forward_body,
        [shape((3, OWN, CELLS), F32)],
        [VMEM] * 2,
        [pltpu.VMEM((ROWS, CELLS), F32)],
        flops=2 * ROWS * CELLS * 256,
        moved=1 << 20,
    )(gathered, filters)[0]
    half = keep + jnp.pad(swapped, ((0, 512 - ROWS), (0, 0)))
    parts = lax.all_to_all(half.reshape(16, 32, 128), "pair", 0, 0)
    mine = jnp.sum(parts, axis=0) * scale
    zs = call(
        adjoint_body,
        [shape((3, OWN, CELLS), F32)],
        [VMEM] * 2,
        [pltpu.VMEM((ROWS, CELLS), F32)],
        flops=2 * ROWS * CELLS * 256,
        moved=1 << 20,
    )(gathered, all_cot)[0]
    from_before = lax.ppermute(jnp.concatenate([ys[0], zs[2]], axis=0), space, up)
    from_after = lax.ppermute(jnp.concatenate([ys[2], zs[0]], axis=0), space, down)
    full = lax.all_to_all(jnp.broadcast_to(mine[None], (16, 32, 128)), "pair", 0, 0)
    full = full.reshape(512, 128)[:ROWS]
    other = lax.ppermute(full, "core", [(0, 1), (1, 0)])
    first = core[0] == 0
    weight_grad = jnp.concatenate(
        [jnp.where(first, full, other), jnp.where(first, other, full)], axis=1
    ).reshape(TAPS, OWN, 256)
    out_field = (ys[1] + from_before[:OWN] + from_after[:OWN]).astype(BF).reshape(field.shape)
    input_grad = (zs[1] + from_before[OWN:] + from_after[OWN:]).astype(BF).reshape(field.shape)
    return out_field, input_grad, weight_grad


def solution(mesh):
    fine = Mesh(mesh.devices.reshape(16, 2, 16), ("pair", "core", "chan"))
    cells = P("chan", ("pair", "core"), None, None)
    taps = P(None, "chan", None)
    return jax.shard_map(
        per_device,
        mesh=fine,
        in_specs=(cells, taps, cells),
        out_specs=(cells, cells, taps),
        check_vma=False,
    )
```

```python
import functools
import math

import jax
import jax.numpy as jnp
from jax import lax
from jax.experimental import pallas as pl
from jax.experimental.pallas import tpu as pltpu
from jax.sharding import Mesh
from jax.sharding import PartitionSpec as P

BF = jnp.bfloat16
F32 = jnp.float32
VMEM = pl.BlockSpec(memory_space=pltpu.VMEM)
TAPS = 27
OWN = 16
CELLS = 1024
ROWS = TAPS * OWN
WIDE = 2 * CELLS + 512
SCALE = 1.0 / math.sqrt(32768)
LIMIT = 48 * 1024 * 1024


def call(body, outs, ins, scratch=(), flops=0, moved=0):
    return pl.pallas_call(
        body,
        out_shape=outs,
        in_specs=ins,
        out_specs=[VMEM] * len(outs),
        scratch_shapes=list(scratch),
        compiler_params=pltpu.CompilerParams(vmem_limit_bytes=LIMIT),
        cost_estimate=pl.CostEstimate(flops=flops, bytes_accessed=moved, transcendentals=0),
    )


def shape(dims, kind):
    return jax.ShapeDtypeStruct(dims, kind)


def lanes(dims):
    return lax.broadcasted_iota(jnp.int32, dims, len(dims) - 1)


def moved_by(block, step):
    if step == 0:
        return block
    at = lanes(block.shape) + step
    turned = pltpu.roll(block, (-step) % 128, 1)
    return jnp.where((at >= 0) & (at < 128), turned, 0.0)


def pack_body(field, cotangent, filters, out):
    for at, rows in ((0, field[...]), (CELLS, cotangent[...])):
        for c in range(16):
            out[c, :, at : at + CELLS] = rows
    lane = lanes((OWN, 128))
    for g in range(4):
        parts = [jnp.zeros((OWN, 128), F32) for _ in range(16)]
        for j in range(8):
            k = 8 * g + j
            if k >= TAPS:
                break
            here = (lane >= 16 * j) & (lane < 16 * j + 16)
            for h in range(2):
                block = filters[k, :, 128 * h : 128 * h + 128].astype(F32)
                for q in range(8):
                    step = (16 * (j - q)) % 128
                    turned = block if step == 0 else pltpu.roll(block, step, 1)
                    parts[8 * h + q] = jnp.where(here, turned, parts[8 * h + q])
        for c in range(16):
            at = 2 * CELLS + 128 * g
            out[c, :, at : at + 128] = parts[c].astype(BF)


def taps_sum(products, a, sign):
    blocks = []
    for r in range(2):
        for z in range(4):
            total = None
            for c in range(3):
                column = None
                for b in range(3):
                    source = z + sign * 2 * (b - 1)
                    if source < 0 or source > 3:
                        continue
                    k = 9 * a + 3 * b + c
                    lane = 128 * (4 * r + source)
                    part = products[16 * k : 16 * k + 16, lane : lane + 128]
                    column = part if column is None else column + part
                column = moved_by(column, sign * 2 * (c - 1))
                total = column if total is None else total + column
            blocks.append(total)
    return blocks


def grad_body(gathered, below, own, above, out, shifted):
    zero = jnp.zeros((OWN, 128), BF)
    for a, source in ((0, above), (1, own), (2, below)):
        for r in range(2):
            rolled = []
            for z in range(4):
                lane = 128 * (4 * r + z)
                block = source[:, lane : lane + 128].astype(F32)
                rolled.append([moved_by(block, -2 * (c - 1)).astype(BF) for c in range(3)])
            for z in range(4):
                for b in range(3):
                    at = z - 2 * (b - 1)
                    for c in range(3):
                        k = 9 * a + 3 * b + c
                        lane = 128 * (4 * r + z)
                        shifted[16 * k : 16 * k + 16, lane : lane + 128] = (
                            rolled[at][c] if 0 <= at < 4 else zero
                        )
    out[0:ROWS, :] = lax.dot_general(
        shifted[...],
        gathered[:, 0:CELLS],
        (((1,), (1,)), ((), ())),
        preferred_element_type=F32,
    )
    out[ROWS:512, :] = jnp.zeros((512 - ROWS, 256), F32)


def sum_body(parts, out):
    total = parts[0]
    for n in range(1, 16):
        total = total + parts[n]
    out[...] = total * SCALE


def share_body(mine, other, out):
    total = mine[...] + other[...]
    for n in range(16):
        out[n] = total


def forward_body(gathered, filters, out, products):
    products[...] = jnp.dot(
        filters[...].reshape(ROWS, 256), gathered[:, 0:CELLS], preferred_element_type=F32
    )
    for a in range(3):
        for n, block in enumerate(taps_sum(products, a, 1)):
            out[a, :, 128 * n : 128 * n + 128] = block


def adjoint_body(gathered, out, products):
    products[...] = lax.dot_general(
        gathered[:, 2 * CELLS : 2 * CELLS + ROWS],
        gathered[:, CELLS : 2 * CELLS],
        (((0,), (0,)), ((), ())),
        preferred_element_type=F32,
    )
    for a in range(3):
        for n, block in enumerate(taps_sum(products, a, -1)):
            out[a, :, 128 * n : 128 * n + 128] = block


def per_device(field, filters, cotangent):
    space = ("pair", "core")
    own_field = field.reshape(OWN, CELLS)
    own_cot = cotangent.reshape(OWN, CELLS)
    up = [(i, i + 1) for i in range(31)]
    down = [(i + 1, i) for i in range(31)]

    packed = call(pack_body, [shape((16, OWN, WIDE), BF)], [VMEM] * 3, moved=1 << 20)(
        own_field, own_cot, filters
    )[0]
    gathered = lax.all_to_all(packed, "chan", 0, 0).reshape(256, WIDE)
    below = lax.ppermute(own_cot, space, up)
    above = lax.ppermute(own_cot, space, down)

    own_grad = call(
        grad_body,
        [shape((512, 256), F32)],
        [VMEM] * 4,
        [pltpu.VMEM((ROWS, CELLS), BF)],
        flops=2 * ROWS * CELLS * 256,
        moved=1 << 20,
    )(gathered, below, own_cot, above)[0]
    parts = lax.all_to_all(own_grad.reshape(16, 32, 256), "pair", 0, 0)
    ys = call(
        forward_body,
        [shape((3, OWN, CELLS), F32)],
        [VMEM] * 2,
        [pltpu.VMEM((ROWS, CELLS), F32)],
        flops=2 * ROWS * CELLS * 256,
        moved=1 << 20,
    )(gathered, filters)[0]
    mine = call(sum_body, [shape((32, 256), F32)], [VMEM], moved=1 << 19)(parts)[0]
    other = lax.ppermute(mine, "core", [(0, 1), (1, 0)])
    shared = call(share_body, [shape((16, 32, 256), F32)], [VMEM] * 2, moved=1 << 19)(mine, other)[0]
    full = lax.all_to_all(shared, "pair", 0, 0)
    zs = call(
        adjoint_body,
        [shape((3, OWN, CELLS), F32)],
        [VMEM],
        [pltpu.VMEM((ROWS, CELLS), F32)],
        flops=2 * ROWS * CELLS * 256,
        moved=1 << 20,
    )(gathered)[0]
    from_before = lax.ppermute(jnp.concatenate([ys[0], zs[2]], axis=0), space, up)
    from_after = lax.ppermute(jnp.concatenate([ys[2], zs[0]], axis=0), space, down)
    out_field = (ys[1] + from_before[:OWN] + from_after[:OWN]).astype(BF).reshape(field.shape)
    input_grad = (zs[1] + from_before[OWN:] + from_after[OWN:]).astype(BF).reshape(field.shape)
    weight_grad = full.reshape(512, 256)[:ROWS].reshape(TAPS, OWN, 256)
    return out_field, input_grad, weight_grad


def solution(mesh):
    fine = Mesh(mesh.devices.reshape(16, 2, 16), ("pair", "core", "chan"))
    cells = P("chan", ("pair", "core"), None, None)
    taps = P(None, "chan", None)
    return jax.shard_map(
        per_device,
        mesh=fine,
        in_specs=(cells, taps, cells),
        out_specs=(cells, cells, taps),
        check_vma=False,
    )
```

```python
import functools
import math

import jax
import jax.numpy as jnp
from jax import lax
from jax.experimental import pallas as pl
from jax.experimental.pallas import tpu as pltpu
from jax.sharding import Mesh
from jax.sharding import PartitionSpec as P

BF = jnp.bfloat16
F32 = jnp.float32
ANY = pl.BlockSpec(memory_space=pl.ANY)
VMEM = pl.BlockSpec(memory_space=pltpu.VMEM)
TAPS = 27
OWN = 16
CELLS = 1024
ROWS = TAPS * OWN
WIDE = 2 * CELLS + 512
SCALE = 1.0 / math.sqrt(32768)
LIMIT = 48 * 1024 * 1024


def call(body, outs, ins, scratch=(), flops=0, moved=0):
    return pl.pallas_call(
        body,
        out_shape=outs,
        in_specs=ins,
        out_specs=[VMEM] * len(outs),
        scratch_shapes=list(scratch),
        compiler_params=pltpu.CompilerParams(vmem_limit_bytes=LIMIT),
        cost_estimate=pl.CostEstimate(flops=flops, bytes_accessed=moved, transcendentals=0),
    )


def shape(dims, kind):
    return jax.ShapeDtypeStruct(dims, kind)


def lanes(dims):
    return lax.broadcasted_iota(jnp.int32, dims, len(dims) - 1)


def moved_by(block, step):
    if step == 0:
        return block
    at = lanes(block.shape) + step
    turned = pltpu.roll(block, (-step) % 128, 1)
    return jnp.where((at >= 0) & (at < 128), turned, 0.0)


def pack_body(field, cotangent, filters, out):
    for at, rows in ((0, field[...]), (CELLS, cotangent[...])):
        for c in range(16):
            out[c, :, at : at + CELLS] = rows
    lane = lanes((OWN, 128))
    for g in range(4):
        parts = [jnp.zeros((OWN, 128), F32) for _ in range(16)]
        for j in range(8):
            k = 8 * g + j
            if k >= TAPS:
                break
            here = (lane >= 16 * j) & (lane < 16 * j + 16)
            for h in range(2):
                block = filters[k, :, 128 * h : 128 * h + 128].astype(F32)
                for q in range(8):
                    step = (16 * (j - q)) % 128
                    turned = block if step == 0 else pltpu.roll(block, step, 1)
                    parts[8 * h + q] = jnp.where(here, turned, parts[8 * h + q])
        for c in range(16):
            at = 2 * CELLS + 128 * g
            out[c, :, at : at + 128] = parts[c].astype(BF)


def taps_sum(products, a, sign):
    blocks = []
    for r in range(2):
        for z in range(4):
            total = None
            for c in range(3):
                column = None
                for b in range(3):
                    source = z + sign * 2 * (b - 1)
                    if source < 0 or source > 3:
                        continue
                    k = 9 * a + 3 * b + c
                    lane = 128 * (4 * r + source)
                    part = products[16 * k : 16 * k + 16, lane : lane + 128]
                    column = part if column is None else column + part
                column = moved_by(column, sign * 2 * (c - 1))
                total = column if total is None else total + column
            blocks.append(total)
    return blocks


def grad_body(gathered, below, own, above, out, shifted):
    zero = jnp.zeros((OWN, 128), BF)
    for a, source in ((0, above), (1, own), (2, below)):
        for r in range(2):
            rolled = []
            for z in range(4):
                lane = 128 * (4 * r + z)
                block = source[:, lane : lane + 128].astype(F32)
                rolled.append([moved_by(block, -2 * (c - 1)).astype(BF) for c in range(3)])
            for z in range(4):
                for b in range(3):
                    at = z - 2 * (b - 1)
                    for c in range(3):
                        k = 9 * a + 3 * b + c
                        lane = 128 * (4 * r + z)
                        shifted[16 * k : 16 * k + 16, lane : lane + 128] = (
                            rolled[at][c] if 0 <= at < 4 else zero
                        )
    out[0:ROWS, :] = lax.dot_general(
        shifted[...],
        gathered[:, 0:CELLS],
        (((1,), (1,)), ((), ())),
        preferred_element_type=F32,
    )
    out[ROWS:512, :] = jnp.zeros((512 - ROWS, 256), F32)


def sum_body(parts, _after, out):
    total = parts[0]
    for n in range(1, 16):
        total = total + parts[n]
    out[...] = total * SCALE


def share_body(both, _after, _too, out):
    total = both[0] + both[1]
    for n in range(16):
        out[n] = total


def contributions_body(gathered, filters, up, down, mid, products):
    products[...] = jnp.dot(
        filters[...].reshape(ROWS, 256), gathered[:, 0:CELLS], preferred_element_type=F32
    )
    for a, out in ((0, up), (1, mid), (2, down)):
        for n, block in enumerate(taps_sum(products, a, 1)):
            out[0:OWN, 128 * n : 128 * n + 128] = block
    products[...] = lax.dot_general(
        gathered[:, 2 * CELLS : 2 * CELLS + ROWS],
        gathered[:, CELLS : 2 * CELLS],
        (((0,), (0,)), ((), ())),
        preferred_element_type=F32,
    )
    for a, out in ((0, down), (1, mid), (2, up)):
        for n, block in enumerate(taps_sum(products, a, -1)):
            out[OWN : 2 * OWN, 128 * n : 128 * n + 128] = block


def per_device(field, filters, cotangent):
    space = ("pair", "core")
    own_field = field.reshape(OWN, CELLS)
    own_cot = cotangent.reshape(OWN, CELLS)
    up = [(i, i + 1) for i in range(31)]
    down = [(i + 1, i) for i in range(31)]

    packed = call(pack_body, [shape((16, OWN, WIDE), BF)], [VMEM] * 3, moved=1 << 20)(
        own_field, own_cot, filters
    )[0]
    gathered = lax.all_to_all(packed, "chan", 0, 0).reshape(256, WIDE)
    below = lax.ppermute(own_cot, space, up)
    above = lax.ppermute(own_cot, space, down)

    own_grad = call(
        grad_body,
        [shape((512, 256), F32)],
        [VMEM] * 4,
        [pltpu.VMEM((ROWS, CELLS), BF)],
        flops=2 * ROWS * CELLS * 256,
        moved=1 << 20,
    )(gathered, below, own_cot, above)[0]
    parts = lax.all_to_all(own_grad.reshape(16, 32, 256), "pair", 0, 0)
    to_next, to_last, own_sums = call(
        contributions_body,
        [shape((2 * OWN, CELLS), F32)] * 3,
        [VMEM] * 2,
        [pltpu.VMEM((ROWS, CELLS), F32)],
        flops=4 * ROWS * CELLS * 256,
        moved=1 << 20,
    )(gathered, filters)
    from_last = lax.ppermute(to_next, space, up)
    from_next = lax.ppermute(to_last, space, down)
    mine = call(sum_body, [shape((32, 256), F32)], [VMEM, ANY], moved=1 << 19)(parts, own_sums)[0]
    both = lax.all_gather(mine, "core", axis=0)
    shared = call(share_body, [shape((16, 32, 256), F32)], [VMEM, ANY, ANY], moved=1 << 19)(
        both, from_last, from_next
    )[0]
    full = lax.all_to_all(shared, "pair", 0, 0)
    outs = (own_sums + from_last + from_next).astype(BF)
    out_field = outs[:OWN].reshape(field.shape)
    input_grad = outs[OWN:].reshape(field.shape)
    weight_grad = full.reshape(512, 256)[:ROWS].reshape(TAPS, OWN, 256)
    return out_field, input_grad, weight_grad


def solution(mesh):
    fine = Mesh(mesh.devices.reshape(16, 2, 16), ("pair", "core", "chan"))
    cells = P("chan", ("pair", "core"), None, None)
    taps = P(None, "chan", None)
    return jax.shard_map(
        per_device,
        mesh=fine,
        in_specs=(cells, taps, cells),
        out_specs=(cells, cells, taps),
        check_vma=False,
    )
```

```python
import functools
import math

import jax
import jax.numpy as jnp
from jax import lax
from jax.experimental import pallas as pl
from jax.experimental.pallas import tpu as pltpu
from jax.sharding import Mesh
from jax.sharding import PartitionSpec as P

BF = jnp.bfloat16
F32 = jnp.float32
HALF = jnp.float16
ANY = pl.BlockSpec(memory_space=pl.ANY)
FAR = pl.BlockSpec(memory_space=pltpu.HBM)
VMEM = pl.BlockSpec(memory_space=pltpu.VMEM)
TAPS = 27
OWN = 16
CELLS = 1024
ROWS = TAPS * OWN
WIDE = 2 * CELLS + 512
SCALE = 1.0 / math.sqrt(32768)
LIMIT = 48 * 1024 * 1024


def call(body, outs, ins, scratch=(), flops=0, moved=0):
    return pl.pallas_call(
        body,
        out_shape=outs,
        in_specs=ins,
        out_specs=[VMEM] * len(outs),
        scratch_shapes=list(scratch),
        compiler_params=pltpu.CompilerParams(vmem_limit_bytes=LIMIT),
        cost_estimate=pl.CostEstimate(flops=flops, bytes_accessed=moved, transcendentals=0),
    )


def shape(dims, kind):
    return jax.ShapeDtypeStruct(dims, kind)


def lanes(dims):
    return lax.broadcasted_iota(jnp.int32, dims, len(dims) - 1)


def moved_by(block, step):
    if step == 0:
        return block
    at = lanes(block.shape) + step
    turned = pltpu.roll(block, (-step) % 128, 1)
    return jnp.where((at >= 0) & (at < 128), turned, 0.0)


def pack_body(field_far, cot_far, filters_far, out, own_cot, field, cotangent, filters, arrived):
    pairs = ((field_far, field), (cot_far, cotangent), (filters_far, filters))
    copies = [pltpu.make_async_copy(a, b, arrived.at[n]) for n, (a, b) in enumerate(pairs)]
    for copy in copies:
        copy.start()
    copies[0].wait()
    copies[1].wait()
    for r in range(2):
        for z in range(4):
            at = 128 * (4 * r + z)
            mine = cotangent[:, r, z, :]
            theirs = field[:, r, z, :]
            own_cot[:, at : at + 128] = mine
            for c in range(16):
                out[c, :, at : at + 128] = theirs
                out[c, :, CELLS + at : CELLS + at + 128] = mine
    copies[2].wait()
    lane = lanes((OWN, 128))
    for g in range(4):
        parts = [jnp.zeros((OWN, 128), F32) for _ in range(16)]
        for j in range(8):
            k = 8 * g + j
            if k >= TAPS:
                break
            here = (lane >= 16 * j) & (lane < 16 * j + 16)
            for h in range(2):
                block = filters[k, :, 128 * h : 128 * h + 128].astype(F32)
                for q in range(8):
                    step = (16 * (j - q)) % 128
                    turned = block if step == 0 else pltpu.roll(block, step, 1)
                    parts[8 * h + q] = jnp.where(here, turned, parts[8 * h + q])
        for c in range(16):
            at = 2 * CELLS + 128 * g
            out[c, :, at : at + 128] = parts[c].astype(BF)


def taps_sum(products, a, sign):
    blocks = []
    for r in range(2):
        for z in range(4):
            total = None
            for c in range(3):
                column = None
                for b in range(3):
                    source = z + sign * 2 * (b - 1)
                    if source < 0 or source > 3:
                        continue
                    k = 9 * a + 3 * b + c
                    lane = 128 * (4 * r + source)
                    part = products[16 * k : 16 * k + 16, lane : lane + 128]
                    column = part if column is None else column + part
                column = moved_by(column, sign * 2 * (c - 1))
                total = column if total is None else total + column
            blocks.append(total)
    return blocks


def grad_body(gathered, below, own, above, out, shifted):
    zero = jnp.zeros((OWN, 128), BF)
    for a, source in ((0, above), (1, own), (2, below)):
        for r in range(2):
            rolled = []
            for z in range(4):
                lane = 128 * (4 * r + z)
                block = source[:, lane : lane + 128].astype(F32)
                rolled.append([moved_by(block, -2 * (c - 1)).astype(BF) for c in range(3)])
            for z in range(4):
                for b in range(3):
                    at = z - 2 * (b - 1)
                    for c in range(3):
                        k = 9 * a + 3 * b + c
                        lane = 128 * (4 * r + z)
                        shifted[16 * k : 16 * k + 16, lane : lane + 128] = (
                            rolled[at][c] if 0 <= at < 4 else zero
                        )
    total = lax.dot_general(
        shifted[...],
        gathered[:, 0:CELLS],
        (((1,), (1,)), ((), ())),
        preferred_element_type=F32,
    )
    power, scaled = scaled_down(total)
    out[...] = jnp.zeros((32, 16, 256), F32)
    for n in range(31):
        rows = min(14, ROWS - 14 * n)
        out[n, 0:rows, :] = scaled[14 * n : 14 * n + rows, :]
        out[n, 14:16, :] = jnp.broadcast_to(power, (2, 256))


def scaled_down(values):
    most = jnp.full((1, 256), jnp.max(jnp.abs(values)), F32)
    power = jnp.ceil(jnp.log2(jnp.maximum(most, 2.0**-100)))
    return power, values * jnp.exp2(14.0 - power)


def sum_body(parts, _after, out):
    total = jnp.zeros((14, 256), F32)
    for n in range(32):
        total = total + parts[n, 0:14, :] * jnp.exp2(parts[n, 14:15, :] - 14.0)
    power, scaled = scaled_down(total * SCALE)
    out[0:14, :] = scaled
    out[14:16, :] = jnp.broadcast_to(power, (2, 256))


def share_body(mine, _after, _too, out):
    out[...] = mine[...]


def finish_body(full, out):
    for n in range(31):
        rows = min(14, ROWS - 14 * n)
        out[14 * n : 14 * n + rows, :] = full[n, 0:rows, :] * jnp.exp2(full[n, 14:15, :] - 14.0)


def contributions_body(gathered, filters, up, down, mid, products):
    products[...] = jnp.dot(
        filters[...].reshape(ROWS, 256), gathered[:, 0:CELLS], preferred_element_type=F32
    )
    for a, out in ((0, up), (1, mid), (2, down)):
        for n, block in enumerate(taps_sum(products, a, 1)):
            out[0:OWN, 128 * n : 128 * n + 128] = block
    products[...] = lax.dot_general(
        gathered[:, 2 * CELLS : 2 * CELLS + ROWS],
        gathered[:, CELLS : 2 * CELLS],
        (((0,), (0,)), ((), ())),
        preferred_element_type=F32,
    )
    for a, out in ((0, down), (1, mid), (2, up)):
        for n, block in enumerate(taps_sum(products, a, -1)):
            out[OWN : 2 * OWN, 128 * n : 128 * n + 128] = block


def per_device(field, filters, cotangent):
    space = ("pair", "core")
    up = [(i, i + 1) for i in range(31)]
    down = [(i + 1, i) for i in range(31)]

    packed, own_cot = call(
        pack_body,
        [shape((16, OWN, WIDE), BF), shape((OWN, CELLS), BF)],
        [FAR] * 3,
        [
            pltpu.VMEM((OWN, 2, 4, 128), BF),
            pltpu.VMEM((OWN, 2, 4, 128), BF),
            pltpu.VMEM((TAPS, OWN, 256), BF),
            pltpu.SemaphoreType.DMA((3,)),
        ],
        moved=1 << 20,
    )(field, cotangent, filters)
    gathered = lax.all_to_all(packed, "chan", 0, 0).reshape(256, WIDE)
    below = lax.ppermute(own_cot, space, up)
    above = lax.ppermute(own_cot, space, down)

    own_grad = call(
        grad_body,
        [shape((32, 16, 256), F32)],
        [VMEM] * 4,
        [pltpu.VMEM((ROWS, CELLS), BF)],
        flops=2 * ROWS * CELLS * 256,
        moved=1 << 20,
    )(gathered, below, own_cot, above)[0]
    parts = lax.all_to_all(own_grad.astype(HALF), space, 0, 0).astype(F32)
    to_next, to_last, own_sums = call(
        contributions_body,
        [shape((2 * OWN, CELLS), F32)] * 3,
        [VMEM] * 2,
        [pltpu.VMEM((ROWS, CELLS), F32)],
        flops=4 * ROWS * CELLS * 256,
        moved=1 << 20,
    )(gathered, filters)
    from_last = lax.ppermute(to_next, space, up)
    from_next = lax.ppermute(to_last, space, down)
    mine = call(sum_body, [shape((16, 256), F32)], [VMEM, ANY], moved=1 << 19)(parts, own_sums)[0]
    shared = call(share_body, [shape((16, 256), F32)], [VMEM, ANY, ANY], moved=1 << 14)(
        mine, from_last, from_next
    )[0]
    shared = jnp.broadcast_to(shared.astype(HALF)[None], (32, 16, 256))
    full = lax.all_to_all(shared, space, 0, 0).astype(F32)
    outs = (own_sums + from_last + from_next).astype(BF)
    out_field = outs[:OWN].reshape(field.shape)
    input_grad = outs[OWN:].reshape(field.shape)
    weight_grad = call(finish_body, [shape((ROWS, 256), F32)], [VMEM], moved=1 << 20)(full)[0]
    weight_grad = weight_grad.reshape(TAPS, OWN, 256)
    return out_field, input_grad, weight_grad


def solution(mesh):
    fine = Mesh(mesh.devices.reshape(16, 2, 16), ("pair", "core", "chan"))
    cells = P("chan", ("pair", "core"), None, None)
    taps = P(None, "chan", None)
    return jax.shard_map(
        per_device,
        mesh=fine,
        in_specs=(cells, taps, cells),
        out_specs=(cells, cells, taps),
        check_vma=False,
    )
```

```python
import functools
import math

import jax
import jax.numpy as jnp
from jax import lax
from jax.experimental import pallas as pl
from jax.experimental.pallas import tpu as pltpu
from jax.sharding import Mesh
from jax.sharding import PartitionSpec as P

BF = jnp.bfloat16
F32 = jnp.float32
HALF = jnp.float16
ANY = pl.BlockSpec(memory_space=pl.ANY)
SMEM = pl.BlockSpec(memory_space=pltpu.SMEM)
FAR = pl.BlockSpec(memory_space=pltpu.HBM)
VMEM = pl.BlockSpec(memory_space=pltpu.VMEM)
TAPS = 27
OWN = 16
CELLS = 1024
ROWS = TAPS * OWN
WIDE = 2 * CELLS + 256
HALF_ROWS = ROWS // 2
SCALE = 1.0 / math.sqrt(32768)
LIMIT = 48 * 1024 * 1024
PACK_LIMIT = 63 * 1024 * 1024
OUTPUTS_FLOPS = 10**10


def call(body, outs, ins, scratch=(), flops=0, moved=0, limit=LIMIT):
    return pl.pallas_call(
        body,
        out_shape=outs,
        in_specs=ins,
        out_specs=[VMEM] * len(outs),
        scratch_shapes=list(scratch),
        compiler_params=pltpu.CompilerParams(vmem_limit_bytes=limit),
        cost_estimate=pl.CostEstimate(flops=flops, bytes_accessed=moved, transcendentals=0),
    )


def shape(dims, kind):
    return jax.ShapeDtypeStruct(dims, kind)


def lanes(dims):
    return lax.broadcasted_iota(jnp.int32, dims, len(dims) - 1)


def moved_by(block, step):
    if step == 0:
        return block
    at = lanes(block.shape) + step
    turned = pltpu.roll(block, (-step) % 128, 1)
    return jnp.where((at >= 0) & (at < 128), turned, 0.0)


def pack_body(
    core, field_far, cot_far, filters_far, out, own_cot, field, cotangent, filters, arrived
):
    pairs = ((field_far, field), (cot_far, cotangent), (filters_far, filters))
    copies = [pltpu.make_async_copy(a, b, arrived.at[n]) for n, (a, b) in enumerate(pairs)]
    for copy in copies:
        copy.start()
    copies[0].wait()
    copies[1].wait()
    for r in range(2):
        for z in range(4):
            at = 128 * (4 * r + z)
            mine = cotangent[:, r, z, :]
            theirs = field[:, r, z, :]
            own_cot[:, at : at + 128] = mine
            for c in range(16):
                out[c, :, at : at + 128] = theirs
                out[c, :, CELLS + at : CELLS + at + 128] = mine
    copies[2].wait()
    lane = lanes((OWN, 128))
    low = core[0] * 11
    for g in range(2):
        parts = [jnp.zeros((OWN, 128), F32) for _ in range(16)]
        for j in range(8):
            here = (lane >= 16 * j) & (lane < 16 * j + 16)
            tap = filters[pl.ds(low + 8 * g + j, 1)][0].astype(F32)
            for h in range(2):
                block = tap[:, 128 * h : 128 * h + 128]
                for q in range(8):
                    step = (16 * (j - q)) % 128
                    turned = block if step == 0 else pltpu.roll(block, step, 1)
                    parts[8 * h + q] = jnp.where(here, turned, parts[8 * h + q])
        for c in range(16):
            at = 2 * CELLS + 128 * g
            out[c, :, at : at + 128] = parts[c].astype(BF)


def taps_sum(products, a, sign):
    blocks = []
    for r in range(2):
        for z in range(4):
            total = None
            for c in range(3):
                column = None
                for b in range(3):
                    source = z + sign * 2 * (b - 1)
                    if source < 0 or source > 3:
                        continue
                    k = 9 * a + 3 * b + c
                    lane = 128 * (4 * r + source)
                    part = products[16 * k : 16 * k + 16, lane : lane + 128]
                    column = part if column is None else column + part
                column = moved_by(column, sign * 2 * (c - 1))
                total = column if total is None else total + column
            blocks.append(total)
    return blocks


def grad_body(core, gathered, below, own, above, keep, send, shifted):
    zero = jnp.zeros((OWN, 128), BF)
    for a, source in ((0, above), (1, own), (2, below)):
        for r in range(2):
            rolled = []
            for z in range(4):
                lane = 128 * (4 * r + z)
                block = source[:, lane : lane + 128].astype(F32)
                rolled.append([moved_by(block, -2 * (c - 1)).astype(BF) for c in range(3)])
            for z in range(4):
                for b in range(3):
                    at = z - 2 * (b - 1)
                    for c in range(3):
                        k = 9 * a + 3 * b + c
                        lane = 128 * (4 * r + z)
                        shifted[16 * k : 16 * k + 16, lane : lane + 128] = (
                            rolled[at][c] if 0 <= at < 4 else zero
                        )
    total = lax.dot_general(
        shifted[...],
        gathered[:, 0:CELLS],
        (((1,), (1,)), ((), ())),
        preferred_element_type=F32,
    )
    first = core[0] == 0
    low, high = total[0:HALF_ROWS], total[HALF_ROWS:ROWS]
    keep[...] = jnp.where(first, low, high)
    send[0:HALF_ROWS, :] = jnp.where(first, high, low)
    send[HALF_ROWS : HALF_ROWS + 256, :] = gathered[:, 2 * CELLS : WIDE].astype(F32)


def chip_body(keep, swapped, out):
    power, scaled = scaled_down(keep[...] + swapped[0:HALF_ROWS, :])
    out[...] = jnp.zeros((16, 16, 256), F32)
    for n in range(16):
        rows = min(14, HALF_ROWS - 14 * n)
        out[n, 0:rows, :] = scaled[14 * n : 14 * n + rows, :]
        out[n, 14:16, :] = jnp.broadcast_to(power, (2, 256))


def scaled_down(values):
    most = jnp.full((1, 256), jnp.max(jnp.abs(values)), F32)
    power = jnp.ceil(jnp.log2(jnp.maximum(most, 2.0**-100)))
    return power, values * jnp.exp2(14.0 - power)


def sum_body(parts, _after, out):
    total = jnp.zeros((14, 256), F32)
    for n in range(16):
        total = total + parts[n, 0:14, :] * jnp.exp2(parts[n, 14:15, :] - 14.0)
    power, scaled = scaled_down(total * SCALE)
    out[0:14, :] = scaled
    out[14:16, :] = jnp.broadcast_to(power, (2, 256))


def finish_body(core, mine, other, out):
    first = core[0] == 0
    for n in range(16):
        rows = min(14, HALF_ROWS - 14 * n)
        ours = mine[n, 0:rows, :] * jnp.exp2(mine[n, 14:15, :] - 14.0)
        theirs = other[n, 0:rows, :] * jnp.exp2(other[n, 14:15, :] - 14.0)
        out[14 * n : 14 * n + rows, :] = jnp.where(first, ours, theirs)
        at = HALF_ROWS + 14 * n
        out[at : at + rows, :] = jnp.where(first, theirs, ours)


def outputs_body(own, last, following, out):
    out[...] = (own[...] + last[...] + following[...]).astype(BF)


def contributions_body(core, gathered, filters, swapped, up, down, mid, products):
    products[...] = jnp.dot(
        filters[...].reshape(ROWS, 256), gathered[:, 0:CELLS], preferred_element_type=F32
    )
    for a, out in ((0, up), (1, mid), (2, down)):
        for n, block in enumerate(taps_sum(products, a, 1)):
            out[0:OWN, 128 * n : 128 * n + 128] = block
    mine = gathered[:, 2 * CELLS : WIDE]
    other = swapped[HALF_ROWS : HALF_ROWS + 256, :].astype(BF)
    first = core[0] == 0
    cells = gathered[:, CELLS : 2 * CELLS]
    over = (((0,), (0,)), ((), ()))
    products[0:256, :] = lax.dot_general(
        jnp.where(first, mine, other), cells, over, preferred_element_type=F32
    )
    products[176:ROWS, :] = lax.dot_general(
        jnp.where(first, other, mine), cells, over, preferred_element_type=F32
    )
    for a, out in ((0, down), (1, mid), (2, up)):
        for n, block in enumerate(taps_sum(products, a, -1)):
            out[OWN : 2 * OWN, 128 * n : 128 * n + 128] = block


def per_device(field, filters, cotangent):
    space = ("pair", "core")
    core = lax.axis_index("core").astype(jnp.int32).reshape(1)
    up = [(i, i + 1) for i in range(31)]
    down = [(i + 1, i) for i in range(31)]
    swap = [(0, 1), (1, 0)]

    packed, own_cot = call(
        pack_body,
        [shape((16, OWN, WIDE), BF), shape((OWN, CELLS), BF)],
        [SMEM] + [FAR] * 3,
        [
            pltpu.VMEM((OWN, 2, 4, 128), BF),
            pltpu.VMEM((OWN, 2, 4, 128), BF),
            pltpu.VMEM((TAPS, OWN, 256), BF),
            pltpu.SemaphoreType.DMA((3,)),
        ],
        moved=1 << 20,
        limit=PACK_LIMIT,
    )(core, field, cotangent, filters)
    gathered = lax.all_to_all(packed, "chan", 0, 0).reshape(256, WIDE)
    below = lax.ppermute(own_cot, space, up)
    above = lax.ppermute(own_cot, space, down)

    keep, send = call(
        grad_body,
        [shape((HALF_ROWS, 256), F32), shape((HALF_ROWS + 256, 256), F32)],
        [SMEM] + [VMEM] * 4,
        [pltpu.VMEM((ROWS, CELLS), BF)],
        flops=2 * ROWS * CELLS * 256,
        moved=1 << 20,
    )(core, gathered, below, own_cot, above)
    swapped = lax.ppermute(send, "core", swap)
    chip = call(chip_body, [shape((16, 16, 256), F32)], [VMEM] * 2, moved=1 << 19)(keep, swapped)[0]
    parts = lax.all_to_all(chip.astype(HALF), "pair", 0, 0).astype(F32)
    to_next, to_last, own_sums = call(
        contributions_body,
        [shape((2 * OWN, CELLS), F32)] * 3,
        [SMEM] + [VMEM] * 3,
        [pltpu.VMEM((ROWS, CELLS), F32)],
        flops=4 * ROWS * CELLS * 256,
        moved=1 << 20,
    )(core, gathered, filters, swapped)
    from_last = lax.ppermute(to_next, space, up)
    from_next = lax.ppermute(to_last, space, down)
    mine = call(sum_body, [shape((16, 256), F32)], [VMEM, ANY], moved=1 << 19)(parts, own_sums)[0]
    spread = jnp.broadcast_to(mine.astype(HALF)[None], (16, 16, 256))
    full = lax.all_to_all(spread, "pair", 0, 0)
    other = lax.ppermute(full, "core", swap)
    weight_grad = call(finish_body, [shape((ROWS, 256), F32)], [SMEM] + [VMEM] * 2, moved=1 << 20)(
        core, full.astype(F32), other.astype(F32)
    )[0]
    outs = call(
        outputs_body, [shape((2 * OWN, CELLS), BF)], [VMEM] * 3, flops=OUTPUTS_FLOPS, moved=1 << 18
    )(own_sums, from_last, from_next)[0]
    out_field = outs[:OWN].reshape(field.shape)
    input_grad = outs[OWN:].reshape(field.shape)
    return out_field, input_grad, weight_grad.reshape(TAPS, OWN, 256)


def solution(mesh):
    fine = Mesh(mesh.devices.reshape(16, 2, 16), ("pair", "core", "chan"))
    cells = P("chan", ("pair", "core"), None, None)
    taps = P(None, "chan", None)
    return jax.shard_map(
        per_device,
        mesh=fine,
        in_specs=(cells, taps, cells),
        out_specs=(cells, cells, taps),
        check_vma=False,
    )
```

```python
import functools
import math

import jax
import jax.numpy as jnp
from jax import lax
from jax.experimental import pallas as pl
from jax.experimental.pallas import tpu as pltpu
from jax.sharding import Mesh
from jax.sharding import PartitionSpec as P

BF = jnp.bfloat16
F32 = jnp.float32
HALF = jnp.float16
ANY = pl.BlockSpec(memory_space=pl.ANY)
SMEM = pl.BlockSpec(memory_space=pltpu.SMEM)
FAR = pl.BlockSpec(memory_space=pltpu.HBM)
VMEM = pl.BlockSpec(memory_space=pltpu.VMEM)
TAPS = 27
OWN = 16
CELLS = 1024
ROWS = TAPS * OWN
WIDE = 2 * CELLS + 256
PART = ROWS // 8
SCALE = 1.0 / math.sqrt(32768)
LIMIT = 16 * 1024 * 1024
PACK_LIMIT = 63 * 1024 * 1024
OUTPUTS_FLOPS = 10**10


def call(body, outs, ins, scratch=(), flops=0, moved=0, limit=LIMIT, outs_at=None):
    return pl.pallas_call(
        body,
        out_shape=outs,
        in_specs=ins,
        out_specs=outs_at or [VMEM] * len(outs),
        scratch_shapes=list(scratch),
        compiler_params=pltpu.CompilerParams(vmem_limit_bytes=limit),
        cost_estimate=pl.CostEstimate(flops=flops, bytes_accessed=moved, transcendentals=0),
    )


def shape(dims, kind):
    return jax.ShapeDtypeStruct(dims, kind)


def lanes(dims):
    return lax.broadcasted_iota(jnp.int32, dims, len(dims) - 1)


def moved_by(block, step):
    if step == 0:
        return block
    at = lanes(block.shape) + step
    turned = pltpu.roll(block, (-step) % 128, 1)
    return jnp.where((at >= 0) & (at < 128), turned, 0.0)


def pack_body(
    core, field_far, cot_far, filters_far, out, own_cot, field, cotangent, filters, cells, taps, arrived, sent
):
    pairs = ((field_far, field), (cot_far, cotangent), (filters_far, filters))
    copies = [pltpu.make_async_copy(a, b, arrived.at[n]) for n, (a, b) in enumerate(pairs)]
    for copy in copies:
        copy.start()
    copies[0].wait()
    copies[1].wait()
    for r in range(2):
        for z in range(4):
            at = 128 * (4 * r + z)
            mine = cotangent[:, r, z, :]
            own_cot[:, at : at + 128] = mine
            cells[:, at : at + 128] = field[:, r, z, :]
            cells[:, CELLS + at : CELLS + at + 128] = mine
    sends = [
        pltpu.make_async_copy(cells, out.at[c, :, pl.ds(0, 2 * CELLS)], sent.at[c]) for c in range(16)
    ]
    for send in sends:
        send.start()
    copies[2].wait()
    lane = lanes((OWN, 128))
    low = core[0] * 11
    for g in range(2):
        parts = [jnp.zeros((OWN, 128), F32) for _ in range(16)]
        for j in range(8):
            here = (lane >= 16 * j) & (lane < 16 * j + 16)
            tap = filters[pl.ds(low + 8 * g + j, 1)][0].astype(F32)
            for h in range(2):
                block = tap[:, 128 * h : 128 * h + 128]
                for q in range(8):
                    step = (16 * (j - q)) % 128
                    turned = block if step == 0 else pltpu.roll(block, step, 1)
                    parts[8 * h + q] = jnp.where(here, turned, parts[8 * h + q])
        for c in range(16):
            taps[c, :, 128 * g : 128 * g + 128] = parts[c].astype(BF)
    last = pltpu.make_async_copy(taps, out.at[:, :, pl.ds(2 * CELLS, 256)], sent.at[16])
    last.start()
    for send in sends:
        send.wait()
    last.wait()


def taps_sum(products, a, sign):
    blocks = []
    for r in range(2):
        for z in range(4):
            total = None
            for c in range(3):
                column = None
                for b in range(3):
                    source = z + sign * 2 * (b - 1)
                    if source < 0 or source > 3:
                        continue
                    k = 9 * a + 3 * b + c
                    lane = 128 * (4 * r + source)
                    part = products[16 * k : 16 * k + 16, lane : lane + 128]
                    column = part if column is None else column + part
                column = moved_by(column, sign * 2 * (c - 1))
                total = column if total is None else total + column
            blocks.append(total)
    return blocks


def grad_body(gathered, below, own, above, out, shifted):
    zero = jnp.zeros((OWN, 128), BF)
    for a, source in ((0, above), (1, own), (2, below)):
        for r in range(2):
            rolled = []
            for z in range(4):
                lane = 128 * (4 * r + z)
                block = source[:, lane : lane + 128].astype(F32)
                rolled.append([moved_by(block, -2 * (c - 1)).astype(BF) for c in range(3)])
            for z in range(4):
                for b in range(3):
                    at = z - 2 * (b - 1)
                    for c in range(3):
                        k = 9 * a + 3 * b + c
                        lane = 128 * (4 * r + z)
                        shifted[16 * k : 16 * k + 16, lane : lane + 128] = (
                            rolled[at][c] if 0 <= at < 4 else zero
                        )
    total = lax.dot_general(
        shifted[...],
        gathered[:, 0:CELLS],
        (((1,), (1,)), ((), ())),
        preferred_element_type=F32,
    )
    power, scaled = scaled_down(total)
    for n in range(8):
        out[n, 0:PART, :] = scaled[PART * n : PART * n + PART, :]
        out[n, PART : PART + 2, :] = jnp.broadcast_to(power, (2, 256))


def scaled_down(values):
    most = jnp.full((1, 256), jnp.max(jnp.abs(values)), F32)
    power = jnp.ceil(jnp.log2(jnp.maximum(most, 2.0**-100)))
    return power, values * jnp.exp2(14.0 - power)


def sum_body(factor, peers, parts, _after, out):
    total = jnp.zeros((PART, 256), F32)
    for n in range(peers):
        total = total + parts[n, 0:PART, :] * jnp.exp2(parts[n, PART : PART + 1, :] - 14.0)
    power, scaled = scaled_down(total * factor)
    out[0:PART, :] = scaled
    out[PART : PART + 2, :] = jnp.broadcast_to(power, (2, 256))


def finish_body(full, out):
    for n in range(8):
        scale = jnp.exp2(full[n, PART : PART + 1, :] - 14.0)
        out[PART * n : PART * n + PART, :] = full[n, 0:PART, :] * scale


def outputs_body(own, near, far, out_field, input_grad):
    for out, at in ((out_field, 0), (input_grad, OWN)):
        for r in range(2):
            for z in range(4):
                here = (slice(at, at + OWN), slice(128 * (4 * r + z), 128 * (4 * r + z) + 128))
                out[:, r, z, :] = (own[here] + near[here] + far[here]).astype(BF)


def contributions_body(core, gathered, filters, swapped, near, far, mid, products):
    first = core[0] == 0
    products[...] = jnp.dot(
        filters[...].reshape(ROWS, 256), gathered[:, 0:CELLS], preferred_element_type=F32
    )
    place(products, 1, first, 0, near, far, mid)
    mine = gathered[:, 2 * CELLS : WIDE]
    other = swapped[...]
    cells = gathered[:, CELLS : 2 * CELLS]
    over = (((0,), (0,)), ((), ()))
    products[0:256, :] = lax.dot_general(
        jnp.where(first, mine, other), cells, over, preferred_element_type=F32
    )
    products[176:ROWS, :] = lax.dot_general(
        jnp.where(first, other, mine), cells, over, preferred_element_type=F32
    )
    place(products, -1, first, OWN, near, far, mid)


def place(products, sign, first, at, near, far, mid):
    following, last = taps_sum(products, 1 - sign, sign), taps_sum(products, 1 + sign, sign)
    for n, block in enumerate(taps_sum(products, 1, sign)):
        here = (slice(at, at + OWN), slice(128 * n, 128 * n + 128))
        mid[here] = block
        near[here] = jnp.where(first, following[n], last[n])
        far[here] = jnp.where(first, last[n], following[n])


def per_device(field, filters, cotangent):
    space = ("far", "near", "core")
    core = lax.axis_index("core").astype(jnp.int32).reshape(1)
    up = [(i, i + 1) for i in range(31)]
    down = [(i + 1, i) for i in range(31)]
    swap = [(0, 1), (1, 0)]
    across = [pair for i in range(1, 31, 2) for pair in ((i, i + 1), (i + 1, i))]

    packed, own_cot = call(
        pack_body,
        [shape((16, OWN, WIDE), BF), shape((OWN, CELLS), BF)],
        [SMEM] + [FAR] * 3,
        [
            pltpu.VMEM((OWN, 2, 4, 128), BF),
            pltpu.VMEM((OWN, 2, 4, 128), BF),
            pltpu.VMEM((TAPS, OWN, 256), BF),
            pltpu.VMEM((OWN, 2 * CELLS), BF),
            pltpu.VMEM((16, OWN, 256), BF),
            pltpu.SemaphoreType.DMA((3,)),
            pltpu.SemaphoreType.DMA((17,)),
        ],
        moved=1 << 20,
        limit=PACK_LIMIT,
        outs_at=[FAR, VMEM],
    )(core, field, cotangent, filters)
    gathered = lax.all_to_all(packed, "chan", 0, 0).reshape(256, WIDE)
    below = lax.ppermute(own_cot, space, up)
    above = lax.ppermute(own_cot, space, down)

    swapped = lax.ppermute(gathered[:, 2 * CELLS :], "core", swap)
    own_grad = call(
        grad_body,
        [shape((8, PART + 2, 256), F32)],
        [VMEM] * 4,
        [pltpu.VMEM((ROWS, CELLS), BF)],
        flops=2 * ROWS * CELLS * 256,
        moved=1 << 20,
    )(gathered, below, own_cot, above)[0]
    parts = lax.all_to_all(own_grad.astype(HALF), ("near", "core"), 0, 0).astype(F32)
    to_near, to_far, own_sums = call(
        contributions_body,
        [shape((2 * OWN, CELLS), F32)] * 3,
        [SMEM] + [VMEM] * 3,
        [pltpu.VMEM((ROWS, CELLS), F32)],
        flops=4 * ROWS * CELLS * 256,
        moved=1 << 20,
    )(core, gathered, filters, swapped)
    from_far = lax.ppermute(to_far, space, across)
    from_near = lax.ppermute(to_near, "core", swap)

    def summed(factor, peers, parts):
        body = functools.partial(sum_body, factor, peers)
        return call(body, [shape((PART + 2, 256), F32)], [VMEM, ANY], moved=1 << 19)(parts, own_sums)[0]

    def spread(part, peers, axes):
        many = jnp.broadcast_to(part.astype(HALF)[None], (peers,) + part.shape)
        return lax.all_to_all(many, axes, 0, 0).astype(F32)

    row = summed(1.0, 8, parts)
    mine = summed(SCALE, 4, spread(row, 4, "far"))
    full = spread(mine, 8, ("near", "core"))
    weight_grad = call(finish_body, [shape((ROWS, 256), F32)], [VMEM], moved=1 << 20)(full)[0]
    out_field, input_grad = call(
        outputs_body, [shape(field.shape, BF)] * 2, [VMEM] * 3, flops=OUTPUTS_FLOPS, moved=1 << 18
    )(own_sums, from_near, from_far)
    return out_field, input_grad, weight_grad.reshape(TAPS, OWN, 256)


def solution(mesh):
    fine = Mesh(mesh.devices.reshape(4, 4, 2, 16), ("far", "near", "core", "chan"))
    cells = P("chan", ("far", "near", "core"), None, None)
    taps = P(None, "chan", None)
    return jax.shard_map(
        per_device,
        mesh=fine,
        in_specs=(cells, taps, cells),
        out_specs=(cells, cells, taps),
        check_vma=False,
    )
```

```python
import functools
import math

import jax
import jax.numpy as jnp
from jax import lax
from jax.experimental import pallas as pl
from jax.experimental.pallas import tpu as pltpu
from jax.sharding import Mesh
from jax.sharding import PartitionSpec as P

BF = jnp.bfloat16
F32 = jnp.float32
HALF = jnp.float16
ANY = pl.BlockSpec(memory_space=pl.ANY)
SMEM = pl.BlockSpec(memory_space=pltpu.SMEM)
FAR = pl.BlockSpec(memory_space=pltpu.HBM)
VMEM = pl.BlockSpec(memory_space=pltpu.VMEM)
TAPS = 27
OWN = 16
CELLS = 1024
ROWS = TAPS * OWN
HALF_CELLS = CELLS // 2
TAPS_AT = CELLS + HALF_CELLS
WIDE = TAPS_AT + 256
PART = ROWS // 8
SCALE = 1.0 / math.sqrt(32768)
LIMIT = 16 * 1024 * 1024
PACK_LIMIT = 63 * 1024 * 1024
CONTRIBUTIONS_FLOPS = 10**10
ROW_FLOPS = 10**9
OUTPUTS_FLOPS = 10**10


def call(body, outs, ins, scratch=(), flops=0, moved=0, limit=LIMIT, outs_at=None):
    return pl.pallas_call(
        body,
        out_shape=outs,
        in_specs=ins,
        out_specs=outs_at or [VMEM] * len(outs),
        scratch_shapes=list(scratch),
        compiler_params=pltpu.CompilerParams(vmem_limit_bytes=limit),
        cost_estimate=pl.CostEstimate(flops=flops, bytes_accessed=moved, transcendentals=0),
    )


def shape(dims, kind):
    return jax.ShapeDtypeStruct(dims, kind)


def lanes(dims):
    return lax.broadcasted_iota(jnp.int32, dims, len(dims) - 1)


def moved_by(block, step):
    if step == 0:
        return block
    at = lanes(block.shape) + step
    turned = pltpu.roll(block, (-step) % 128, 1)
    return jnp.where((at >= 0) & (at < 128), turned, 0.0)


def pack_body(
    core_at, side_at, field_far, cot_far, filters_far, out, own_cot, field, cotangent, filters, cells, taps, arrived, sent
):
    core, side = core_at[0], side_at[0]
    pairs = ((field_far, field), (cot_far, cotangent), (filters_far, filters))
    copies = [pltpu.make_async_copy(a, b, arrived.at[n]) for n, (a, b) in enumerate(pairs)]
    for copy in copies:
        copy.start()
    copies[0].wait()
    copies[1].wait()
    for r in range(2):
        for z in range(4):
            at = 128 * (4 * r + z)
            mine = cotangent[:, r, z, :]
            own_cot[:, at : at + 128] = mine
            cells[0, :, at : at + 128] = field[:, r, z, :]
            cells[1, :, at : at + 128] = field[:, r, z, :]
            at = CELLS + 128 * z
            cells[jnp.where(side == r, 0, 1), :, at : at + 128] = mine
    sends = [
        pltpu.make_async_copy(cells.at[c // 8], out.at[c, :, pl.ds(0, TAPS_AT)], sent.at[c])
        for c in range(16)
    ]
    for send in sends:
        send.start()
    copies[2].wait()
    lane = lanes((OWN, 128))
    low = core * 11
    for g in range(2):
        parts = [jnp.zeros((OWN, 128), F32) for _ in range(16)]
        for j in range(8):
            here = (lane >= 16 * j) & (lane < 16 * j + 16)
            tap = filters[pl.ds(low + 8 * g + j, 1)][0].astype(F32)
            for h in range(2):
                block = tap[:, 128 * h : 128 * h + 128]
                for q in range(8):
                    step = (16 * (j - q)) % 128
                    turned = block if step == 0 else pltpu.roll(block, step, 1)
                    parts[8 * h + q] = jnp.where(here, turned, parts[8 * h + q])
        for c in range(16):
            taps[c, :, 128 * g : 128 * g + 128] = parts[c].astype(BF)
    last = pltpu.make_async_copy(taps, out.at[:, :, pl.ds(TAPS_AT, 256)], sent.at[16])
    last.start()
    for send in sends:
        send.wait()
    last.wait()


def taps_sum(products, a, sign):
    blocks = []
    for r in range(2):
        for z in range(4):
            total = None
            for c in range(3):
                column = None
                for b in range(3):
                    source = z + sign * 2 * (b - 1)
                    if source < 0 or source > 3:
                        continue
                    k = 9 * a + 3 * b + c
                    lane = 128 * (4 * r + source)
                    part = products[16 * k : 16 * k + 16, lane : lane + 128]
                    column = part if column is None else column + part
                column = moved_by(column, sign * 2 * (c - 1))
                total = column if total is None else total + column
            blocks.append(total)
    return blocks


def grad_body(gathered, below, own, above, out, shifted):
    zero = jnp.zeros((OWN, 128), BF)
    for a, source in ((0, above), (1, own), (2, below)):
        for r in range(2):
            rolled = []
            for z in range(4):
                lane = 128 * (4 * r + z)
                block = source[:, lane : lane + 128].astype(F32)
                rolled.append([moved_by(block, -2 * (c - 1)).astype(BF) for c in range(3)])
            for z in range(4):
                for b in range(3):
                    at = z - 2 * (b - 1)
                    for c in range(3):
                        k = 9 * a + 3 * b + c
                        lane = 128 * (4 * r + z)
                        shifted[16 * k : 16 * k + 16, lane : lane + 128] = (
                            rolled[at][c] if 0 <= at < 4 else zero
                        )
    total = lax.dot_general(
        shifted[...],
        gathered[:, 0:CELLS],
        (((1,), (1,)), ((), ())),
        preferred_element_type=F32,
    )
    power, scaled = scaled_down(total)
    for n in range(8):
        out[n, 0:PART, :] = scaled[PART * n : PART * n + PART, :]
        out[n, PART : PART + 2, :] = jnp.broadcast_to(power, (2, 256))


def parts_body(gathered, _after, cells, taps):
    cells[...] = gathered[:, CELLS:TAPS_AT]
    taps[...] = gathered[:, TAPS_AT:WIDE]


def scaled_down(values):
    most = jnp.full((1, 256), jnp.max(jnp.abs(values)), F32)
    power = jnp.ceil(jnp.log2(jnp.maximum(most, 2.0**-100)))
    return power, values * jnp.exp2(14.0 - power)


def sum_body(factor, peers, parts, *rest):
    out = rest[-1]
    total = jnp.zeros((PART, 256), F32)
    for n in range(peers):
        total = total + parts[n, 0:PART, :] * jnp.exp2(parts[n, PART : PART + 1, :] - 14.0)
    power, scaled = scaled_down(total * factor)
    out[0:PART, :] = scaled
    out[PART : PART + 2, :] = jnp.broadcast_to(power, (2, 256))


def finish_body(full, out):
    for n in range(8):
        scale = jnp.exp2(full[n, PART : PART + 1, :] - 14.0)
        out[PART * n : PART * n + PART, :] = full[n, 0:PART, :] * scale


def outputs_body(own, near, far, out_field, input_grad):
    for out, at in ((out_field, 0), (input_grad, OWN)):
        for r in range(2):
            for z in range(4):
                here = (slice(at, at + OWN), slice(128 * (4 * r + z), 128 * (4 * r + z) + 128))
                out[:, r, z, :] = (own[here] + near[here] + far[here]).astype(BF)


def contributions_body(core, side_at, gathered, filters, swapped, halves, near, far, mid, products):
    first, side = core[0] == 0, side_at[0]
    products[...] = jnp.dot(
        filters[...].reshape(ROWS, 256), gathered[:, 0:CELLS], preferred_element_type=F32
    )
    put(products, 1, first, 0, near, far, mid)
    mine = gathered[:, TAPS_AT:WIDE]
    other = swapped[...]
    low, high = jnp.where(first, mine, other), jnp.where(first, other, mine)
    over = (((0,), (0,)), ((), ()))
    for r in range(2):
        rows = []
        for line in range(2):
            here = slice(128 * line, 128 * line + 128)
            kept = (side == line) if r == 0 else (side != line)
            rows.append(jnp.where(kept, gathered[here, CELLS:TAPS_AT], halves[here, :]))
        cells = jnp.concatenate(rows, axis=0)
        at = slice(HALF_CELLS * r, HALF_CELLS * r + HALF_CELLS)
        products[0:256, at] = lax.dot_general(low, cells, over, preferred_element_type=F32)
        products[176:ROWS, at] = lax.dot_general(high, cells, over, preferred_element_type=F32)
    put(products, -1, first, OWN, near, far, mid)


def put(products, sign, first, at, near, far, mid):
    following, last = taps_sum(products, 1 - sign, sign), taps_sum(products, 1 + sign, sign)
    for n, block in enumerate(taps_sum(products, 1, sign)):
        here = (slice(at, at + OWN), slice(128 * n, 128 * n + 128))
        mid[here] = block
        near[here] = jnp.where(first, following[n], last[n])
        far[here] = jnp.where(first, last[n], following[n])


def per_device(field, filters, cotangent):
    space = ("far", "near", "core")
    chan = ("side", "line")
    core, side = (lax.axis_index(name).astype(jnp.int32).reshape(1) for name in ("core", "side"))
    up = [(i, i + 1) for i in range(31)]
    down = [(i + 1, i) for i in range(31)]
    swap = [(0, 1), (1, 0)]
    across = [pair for i in range(1, 31, 2) for pair in ((i, i + 1), (i + 1, i))]

    packed, own_cot = call(
        pack_body,
        [shape((16, OWN, WIDE), BF), shape((OWN, CELLS), BF)],
        [SMEM] * 2 + [FAR] * 3,
        [
            pltpu.VMEM((OWN, 2, 4, 128), BF),
            pltpu.VMEM((OWN, 2, 4, 128), BF),
            pltpu.VMEM((TAPS, OWN, 256), BF),
            pltpu.VMEM((2, OWN, TAPS_AT), BF),
            pltpu.VMEM((16, OWN, 256), BF),
            pltpu.SemaphoreType.DMA((3,)),
            pltpu.SemaphoreType.DMA((17,)),
        ],
        moved=1 << 20,
        limit=PACK_LIMIT,
        outs_at=[FAR, VMEM],
    )(core, side, field, cotangent, filters)
    gathered = lax.all_to_all(packed, chan, 0, 0).reshape(256, WIDE)
    below = lax.ppermute(own_cot, space, up)
    above = lax.ppermute(own_cot, space, down)

    own_grad = call(
        grad_body,
        [shape((8, PART + 2, 256), F32)],
        [VMEM] * 4,
        [pltpu.VMEM((ROWS, CELLS), BF)],
        flops=2 * ROWS * CELLS * 256,
        moved=1 << 20,
    )(gathered, below, own_cot, above)[0]
    half_cells, half_taps = call(
        parts_body, [shape((256, HALF_CELLS), BF), shape((256, 256), BF)], [VMEM, ANY], moved=1 << 19
    )(gathered, own_grad)
    halves = lax.ppermute(half_cells, "side", swap)
    swapped = lax.ppermute(half_taps, "core", swap)
    parts = lax.all_to_all(own_grad.astype(HALF), ("near", "core"), 0, 0).astype(F32)
    to_near, to_far, own_sums = call(
        contributions_body,
        [shape((2 * OWN, CELLS), F32)] * 3,
        [SMEM] * 2 + [VMEM] * 4,
        [pltpu.VMEM((ROWS, CELLS), F32)],
        flops=CONTRIBUTIONS_FLOPS,
        moved=1 << 20,
    )(core, side, gathered, filters, swapped, halves)
    from_far = lax.ppermute(to_far, space, across)
    from_near = lax.ppermute(to_near, "core", swap)

    def summed(factor, peers, flops, parts, *after):
        body = functools.partial(sum_body, factor, peers)
        return call(body, [shape((PART + 2, 256), F32)], [VMEM] + [ANY] * len(after), flops=flops)(
            parts, *after
        )[0]

    def spread(part, peers, axes):
        many = jnp.broadcast_to(part.astype(HALF)[None], (peers,) + part.shape)
        return lax.all_to_all(many, axes, 0, 0).astype(F32)

    row = summed(1.0, 8, ROW_FLOPS, parts)
    mine = summed(SCALE, 4, 0, spread(row, 4, "far"), own_sums)
    full = spread(mine, 8, ("near", "core"))
    weight_grad = call(finish_body, [shape((ROWS, 256), F32)], [VMEM], moved=1 << 20)(full)[0]
    out_field, input_grad = call(
        outputs_body, [shape(field.shape, BF)] * 2, [VMEM] * 3, flops=OUTPUTS_FLOPS, moved=1 << 18
    )(own_sums, from_near, from_far)
    return out_field, input_grad, weight_grad.reshape(TAPS, OWN, 256)


def solution(mesh):
    fine = Mesh(mesh.devices.reshape(4, 4, 2, 2, 8), ("far", "near", "core", "side", "line"))
    cells = P(("side", "line"), ("far", "near", "core"), None, None)
    taps = P(None, ("side", "line"), None)
    return jax.shard_map(
        per_device,
        mesh=fine,
        in_specs=(cells, taps, cells),
        out_specs=(cells, cells, taps),
        check_vma=False,
    )
```

```python
import functools
import math

import jax
import jax.numpy as jnp
from jax import lax
from jax.experimental import pallas as pl
from jax.experimental.pallas import tpu as pltpu
from jax.sharding import Mesh
from jax.sharding import PartitionSpec as P

BF = jnp.bfloat16
F32 = jnp.float32
HALF = jnp.float16
ANY = pl.BlockSpec(memory_space=pl.ANY)
SMEM = pl.BlockSpec(memory_space=pltpu.SMEM)
FAR = pl.BlockSpec(memory_space=pltpu.HBM)
VMEM = pl.BlockSpec(memory_space=pltpu.VMEM)
TAPS = 27
OWN = 16
CELLS = 1024
ROWS = TAPS * OWN
HALF_CELLS = CELLS // 2
TAPS_AT = CELLS + HALF_CELLS
WIDE = TAPS_AT + 256
PART = ROWS // 8
SCALE = 1.0 / math.sqrt(32768)
LIMIT = 16 * 1024 * 1024
PACK_LIMIT = 63 * 1024 * 1024
CONTRIBUTIONS_FLOPS = 10**10
ROW_FLOPS = 10**9
FAR_FLOPS = 15 * 10**8


def call(body, outs, ins, scratch=(), flops=0, moved=0, limit=LIMIT, outs_at=None):
    return pl.pallas_call(
        body,
        out_shape=outs,
        in_specs=ins,
        out_specs=outs_at or [VMEM] * len(outs),
        scratch_shapes=list(scratch),
        compiler_params=pltpu.CompilerParams(vmem_limit_bytes=limit),
        cost_estimate=pl.CostEstimate(flops=flops, bytes_accessed=moved, transcendentals=0),
    )


def shape(dims, kind):
    return jax.ShapeDtypeStruct(dims, kind)


def lanes(dims):
    return lax.broadcasted_iota(jnp.int32, dims, len(dims) - 1)


def moved_by(block, step):
    if step == 0:
        return block
    at = lanes(block.shape) + step
    turned = pltpu.roll(block, (-step) % 128, 1)
    return jnp.where((at >= 0) & (at < 128), turned, 0.0)


def pack_body(
    core_at, side_at, field_far, cot_far, filters_far, out, own_cot, field, cotangent, filters, cells, taps, arrived, sent
):
    core, side = core_at[0], side_at[0]
    own_taps = filters_far.at[pl.ds(11 * core, 16)]
    pairs = ((field_far, field), (cot_far, cotangent), (own_taps, filters))
    copies = [pltpu.make_async_copy(a, b, arrived.at[n]) for n, (a, b) in enumerate(pairs)]
    for copy in copies:
        copy.start()
    copies[0].wait()
    copies[1].wait()
    for r in range(2):
        for z in range(4):
            at = 128 * (4 * r + z)
            mine = cotangent[:, r, z, :]
            own_cot[:, at : at + 128] = mine
            cells[0, :, at : at + 128] = field[:, r, z, :]
            cells[1, :, at : at + 128] = field[:, r, z, :]
            at = CELLS + 128 * z
            cells[jnp.where(side == r, 0, 1), :, at : at + 128] = mine
    sends = [
        pltpu.make_async_copy(cells.at[c // 8], out.at[c, :, pl.ds(0, TAPS_AT)], sent.at[c])
        for c in range(16)
    ]
    for send in sends:
        send.start()
    copies[2].wait()
    lane = lanes((OWN, 128))
    for g in range(2):
        parts = [jnp.zeros((OWN, 128), F32) for _ in range(16)]
        for j in range(8):
            here = (lane >= 16 * j) & (lane < 16 * j + 16)
            tap = filters[8 * g + j].astype(F32)
            for h in range(2):
                block = tap[:, 128 * h : 128 * h + 128]
                for q in range(8):
                    step = (16 * (j - q)) % 128
                    turned = block if step == 0 else pltpu.roll(block, step, 1)
                    parts[8 * h + q] = jnp.where(here, turned, parts[8 * h + q])
        for c in range(16):
            taps[c, :, 128 * g : 128 * g + 128] = parts[c].astype(BF)
    last = pltpu.make_async_copy(taps, out.at[:, :, pl.ds(TAPS_AT, 256)], sent.at[16])
    last.start()
    for send in sends:
        send.wait()
    last.wait()


def taps_sum(products, a, sign):
    blocks = []
    for r in range(2):
        for z in range(4):
            total = None
            for c in range(3):
                column = None
                for b in range(3):
                    source = z + sign * 2 * (b - 1)
                    if source < 0 or source > 3:
                        continue
                    k = 9 * a + 3 * b + c
                    lane = 128 * (4 * r + source)
                    part = products[16 * k : 16 * k + 16, lane : lane + 128]
                    column = part if column is None else column + part
                column = moved_by(column, sign * 2 * (c - 1))
                total = column if total is None else total + column
            blocks.append(total)
    return blocks


def grad_body(gathered, below, own, above, out, shifted):
    zero = jnp.zeros((OWN, 128), BF)
    for a, source in ((0, above), (1, own), (2, below)):
        for r in range(2):
            rolled = []
            for z in range(4):
                lane = 128 * (4 * r + z)
                block = source[:, lane : lane + 128].astype(F32)
                rolled.append([moved_by(block, -2 * (c - 1)).astype(BF) for c in range(3)])
            for z in range(4):
                for b in range(3):
                    at = z - 2 * (b - 1)
                    for c in range(3):
                        k = 9 * a + 3 * b + c
                        lane = 128 * (4 * r + z)
                        shifted[16 * k : 16 * k + 16, lane : lane + 128] = (
                            rolled[at][c] if 0 <= at < 4 else zero
                        )
    total = lax.dot_general(
        shifted[...],
        gathered[:, 0:CELLS],
        (((1,), (1,)), ((), ())),
        preferred_element_type=F32,
    )
    power, scaled = scaled_down(total)
    for n in range(8):
        out[n, 0:PART, :] = scaled[PART * n : PART * n + PART, :]
        out[n, PART : PART + 2, :] = jnp.broadcast_to(power, (2, 256))


def parts_body(gathered, _after, cells, taps):
    cells[...] = gathered[:, CELLS:TAPS_AT]
    taps[...] = gathered[:, TAPS_AT:WIDE]


def scaled_down(values):
    most = jnp.full((1, 256), jnp.max(jnp.abs(values)), F32)
    power = jnp.ceil(jnp.log2(jnp.maximum(most, 2.0**-100)))
    return power, values * jnp.exp2(14.0 - power)


def sum_body(factor, peers, parts, *rest):
    out = rest[-1]
    total = jnp.zeros((PART, 256), F32)
    for n in range(peers):
        total = total + parts[n, 0:PART, :] * jnp.exp2(parts[n, PART : PART + 1, :] - 14.0)
    power, scaled = scaled_down(total * factor)
    out[0:PART, :] = scaled
    out[PART : PART + 2, :] = jnp.broadcast_to(power, (2, 256))


def finish_body(full, out_far, out, sent):
    half = ROWS // 2
    copies = []
    for h in range(2):
        for n in range(4 * h, 4 * h + 4):
            scale = jnp.exp2(full[n, PART : PART + 1, :] - 14.0)
            out[PART * n : PART * n + PART, :] = full[n, 0:PART, :] * scale
        here = pl.ds(half * h, half)
        copies.append(pltpu.make_async_copy(out.at[here], out_far.at[here], sent.at[h]))
        copies[h].start()
    for copy in copies:
        copy.wait()


def far_body(own, far, out):
    out[...] = own[...] + far[...]


def outputs_body(own, near, out_field, input_grad):
    for out, at in ((out_field, 0), (input_grad, OWN)):
        for r in range(2):
            for z in range(4):
                here = (slice(at, at + OWN), slice(128 * (4 * r + z), 128 * (4 * r + z) + 128))
                out[:, r, z, :] = (own[here] + near[here]).astype(BF)


def contributions_body(core, side_at, gathered, filters, swapped, halves, near, far, mid, products):
    first, side = core[0] == 0, side_at[0]
    products[...] = jnp.dot(
        filters[...].reshape(ROWS, 256), gathered[:, 0:CELLS], preferred_element_type=F32
    )
    put(products, 1, first, 0, near, far, mid)
    mine = gathered[:, TAPS_AT:WIDE]
    other = swapped[...]
    low, high = jnp.where(first, mine, other), jnp.where(first, other, mine)
    over = (((0,), (0,)), ((), ()))
    for r in range(2):
        rows = []
        for line in range(2):
            here = slice(128 * line, 128 * line + 128)
            kept = (side == line) if r == 0 else (side != line)
            rows.append(jnp.where(kept, gathered[here, CELLS:TAPS_AT], halves[here, :]))
        cells = jnp.concatenate(rows, axis=0)
        at = slice(HALF_CELLS * r, HALF_CELLS * r + HALF_CELLS)
        products[0:256, at] = lax.dot_general(low, cells, over, preferred_element_type=F32)
        products[176:ROWS, at] = lax.dot_general(high, cells, over, preferred_element_type=F32)
    put(products, -1, first, OWN, near, far, mid)


def put(products, sign, first, at, near, far, mid):
    following, last = taps_sum(products, 1 - sign, sign), taps_sum(products, 1 + sign, sign)
    for n, block in enumerate(taps_sum(products, 1, sign)):
        here = (slice(at, at + OWN), slice(128 * n, 128 * n + 128))
        mid[here] = block
        near[here] = jnp.where(first, following[n], last[n])
        far[here] = jnp.where(first, last[n], following[n])


def per_device(field, filters, cotangent):
    space = ("far", "near", "core")
    chan = ("side", "line")
    core, side = (lax.axis_index(name).astype(jnp.int32).reshape(1) for name in ("core", "side"))
    up = [(i, i + 1) for i in range(31)]
    down = [(i + 1, i) for i in range(31)]
    swap = [(0, 1), (1, 0)]
    across = [pair for i in range(1, 31, 2) for pair in ((i, i + 1), (i + 1, i))]

    packed, own_cot = call(
        pack_body,
        [shape((16, OWN, WIDE), BF), shape((OWN, CELLS), BF)],
        [SMEM] * 2 + [FAR] * 3,
        [
            pltpu.VMEM((OWN, 2, 4, 128), BF),
            pltpu.VMEM((OWN, 2, 4, 128), BF),
            pltpu.VMEM((16, OWN, 256), BF),
            pltpu.VMEM((2, OWN, TAPS_AT), BF),
            pltpu.VMEM((16, OWN, 256), BF),
            pltpu.SemaphoreType.DMA((3,)),
            pltpu.SemaphoreType.DMA((17,)),
        ],
        moved=1 << 20,
        limit=PACK_LIMIT,
        outs_at=[FAR, VMEM],
    )(core, side, field, cotangent, filters)
    gathered = lax.all_to_all(packed, chan, 0, 0).reshape(256, WIDE)
    below = lax.ppermute(own_cot, space, up)
    above = lax.ppermute(own_cot, space, down)

    own_grad = call(
        grad_body,
        [shape((8, PART + 2, 256), F32)],
        [VMEM] * 4,
        [pltpu.VMEM((ROWS, CELLS), BF)],
        flops=2 * ROWS * CELLS * 256,
        moved=1 << 20,
    )(gathered, below, own_cot, above)[0]
    half_cells, half_taps = call(
        parts_body, [shape((256, HALF_CELLS), BF), shape((256, 256), BF)], [VMEM, ANY], moved=1 << 19
    )(gathered, own_grad)
    halves = lax.ppermute(half_cells, "side", swap)
    swapped = lax.ppermute(half_taps, "core", swap)
    parts = lax.all_to_all(own_grad.astype(HALF), ("near", "core"), 0, 0).astype(F32)
    to_near, to_far, own_sums = call(
        contributions_body,
        [shape((2 * OWN, CELLS), F32)] * 3,
        [SMEM] * 2 + [VMEM] * 4,
        [pltpu.VMEM((ROWS, CELLS), F32)],
        flops=CONTRIBUTIONS_FLOPS,
        moved=1 << 20,
    )(core, side, gathered, filters, swapped, halves)
    from_far = lax.ppermute(to_far, space, across)

    def summed(factor, peers, flops, parts, *after):
        body = functools.partial(sum_body, factor, peers)
        return call(body, [shape((PART + 2, 256), F32)], [VMEM] + [ANY] * len(after), flops=flops)(
            parts, *after
        )[0]

    def spread(part, peers, axes):
        many = jnp.broadcast_to(part.astype(HALF)[None], (peers,) + part.shape)
        return lax.all_to_all(many, axes, 0, 0).astype(F32)

    row = summed(1.0, 8, ROW_FLOPS, parts)
    mine = summed(SCALE, 4, 0, spread(row, 4, "far"), own_sums)
    from_near = lax.ppermute(to_near, "core", swap)
    full = spread(mine, 8, ("near", "core"))
    weight_grad = call(
        finish_body,
        [shape((ROWS, 256), F32)],
        [VMEM],
        [pltpu.VMEM((ROWS, 256), F32), pltpu.SemaphoreType.DMA((2,))],
        moved=1 << 20,
        outs_at=[FAR],
    )(full)[0]
    own_and_far = call(far_body, [shape((2 * OWN, CELLS), F32)], [VMEM] * 2, flops=FAR_FLOPS)(
        own_sums, from_far
    )[0]
    out_field, input_grad = call(outputs_body, [shape(field.shape, BF)] * 2, [VMEM] * 2, moved=1 << 18)(
        own_and_far, from_near
    )
    return out_field, input_grad, weight_grad.reshape(TAPS, OWN, 256)


def solution(mesh):
    fine = Mesh(mesh.devices.reshape(4, 4, 2, 2, 8), ("far", "near", "core", "side", "line"))
    cells = P(("side", "line"), ("far", "near", "core"), None, None)
    taps = P(None, ("side", "line"), None)
    return jax.shard_map(
        per_device,
        mesh=fine,
        in_specs=(cells, taps, cells),
        out_specs=(cells, cells, taps),
        check_vma=False,
    )
```

```python
import functools
import math

import jax
import jax.numpy as jnp
from jax import lax
from jax.experimental import pallas as pl
from jax.experimental.pallas import tpu as pltpu
from jax.sharding import Mesh
from jax.sharding import PartitionSpec as P

BF = jnp.bfloat16
F32 = jnp.float32
HALF = jnp.float16
ANY = pl.BlockSpec(memory_space=pl.ANY)
SMEM = pl.BlockSpec(memory_space=pltpu.SMEM)
FAR = pl.BlockSpec(memory_space=pltpu.HBM)
VMEM = pl.BlockSpec(memory_space=pltpu.VMEM)
TAPS = 27
OWN = 16
CELLS = 1024
ROWS = TAPS * OWN
HALF_CELLS = CELLS // 2
TAPS_AT = CELLS + HALF_CELLS
WIDE = TAPS_AT + 256
PART = ROWS // 8
SCALE = 1.0 / math.sqrt(32768)
LIMIT = 16 * 1024 * 1024
PACK_LIMIT = 63 * 1024 * 1024
CONTRIBUTIONS_FLOPS = 10**10
ROW_FLOPS = 10**9
FAR_FLOPS = 15 * 10**8


def call(body, outs, ins, scratch=(), flops=0, moved=0, limit=LIMIT, outs_at=None):
    return pl.pallas_call(
        body,
        out_shape=outs,
        in_specs=ins,
        out_specs=outs_at or [VMEM] * len(outs),
        scratch_shapes=list(scratch),
        compiler_params=pltpu.CompilerParams(vmem_limit_bytes=limit),
        cost_estimate=pl.CostEstimate(flops=flops, bytes_accessed=moved, transcendentals=0),
    )


def shape(dims, kind):
    return jax.ShapeDtypeStruct(dims, kind)


def lanes(dims):
    return lax.broadcasted_iota(jnp.int32, dims, len(dims) - 1)


def moved_by(block, step):
    if step == 0:
        return block
    at = lanes(block.shape) + step
    turned = pltpu.roll(block, (-step) % 128, 1)
    return jnp.where((at >= 0) & (at < 128), turned, 0.0)


def pack_body(
    core_at, side_at, field_far, cot_far, filters_far, out, own_cot, field, cotangent, filters, cells, taps, arrived, sent
):
    core, side = core_at[0], side_at[0]
    own_taps = filters_far.at[pl.ds(11 * core, 16)]
    pairs = ((field_far, field), (cot_far, cotangent), (own_taps, filters))
    copies = [pltpu.make_async_copy(a, b, arrived.at[n]) for n, (a, b) in enumerate(pairs)]
    for copy in copies:
        copy.start()
    copies[0].wait()
    copies[1].wait()
    for r in range(2):
        for z in range(4):
            at = 128 * (4 * r + z)
            mine = cotangent[:, r, z, :]
            own_cot[:, at : at + 128] = mine
            cells[0, :, at : at + 128] = field[:, r, z, :]
            cells[1, :, at : at + 128] = field[:, r, z, :]
            at = CELLS + 128 * z
            cells[jnp.where(side == r, 0, 1), :, at : at + 128] = mine
    sends = [
        pltpu.make_async_copy(cells.at[c // 8], out.at[c, :, pl.ds(0, TAPS_AT)], sent.at[c])
        for c in range(16)
    ]
    for send in sends:
        send.start()
    copies[2].wait()
    lane = lanes((OWN, 128))
    for g in range(2):
        parts = [jnp.zeros((OWN, 128), F32) for _ in range(16)]
        for j in range(8):
            here = (lane >= 16 * j) & (lane < 16 * j + 16)
            tap = filters[8 * g + j].astype(F32)
            for h in range(2):
                block = tap[:, 128 * h : 128 * h + 128]
                for q in range(8):
                    step = (16 * (j - q)) % 128
                    turned = block if step == 0 else pltpu.roll(block, step, 1)
                    parts[8 * h + q] = jnp.where(here, turned, parts[8 * h + q])
        for c in range(16):
            taps[c, :, 128 * g : 128 * g + 128] = parts[c].astype(BF)
    last = pltpu.make_async_copy(taps, out.at[:, :, pl.ds(TAPS_AT, 256)], sent.at[16])
    last.start()
    for send in sends:
        send.wait()
    last.wait()


def taps_sum(products, a, sign):
    blocks = []
    for r in range(2):
        for z in range(4):
            total = None
            for c in range(3):
                column = None
                for b in range(3):
                    source = z + sign * 2 * (b - 1)
                    if source < 0 or source > 3:
                        continue
                    k = 9 * a + 3 * b + c
                    lane = 128 * (4 * r + source)
                    part = products[16 * k : 16 * k + 16, lane : lane + 128]
                    column = part if column is None else column + part
                column = moved_by(column, sign * 2 * (c - 1))
                total = column if total is None else total + column
            blocks.append(total)
    return blocks


def grad_body(gathered, below, own, above, out, shifted):
    zero = jnp.zeros((OWN, 128), BF)
    for a, source in ((0, above), (1, own), (2, below)):
        for r in range(2):
            rolled = []
            for z in range(4):
                lane = 128 * (4 * r + z)
                block = source[:, lane : lane + 128].astype(F32)
                rolled.append([moved_by(block, -2 * (c - 1)).astype(BF) for c in range(3)])
            for z in range(4):
                for b in range(3):
                    at = z - 2 * (b - 1)
                    for c in range(3):
                        k = 9 * a + 3 * b + c
                        lane = 128 * (4 * r + z)
                        shifted[16 * k : 16 * k + 16, lane : lane + 128] = (
                            rolled[at][c] if 0 <= at < 4 else zero
                        )
    total = lax.dot_general(
        shifted[...],
        gathered[:, 0:CELLS],
        (((1,), (1,)), ((), ())),
        preferred_element_type=F32,
    )
    power, scaled = scaled_down(total)
    for n in range(8):
        out[n, 0:PART, :] = scaled[PART * n : PART * n + PART, :]
        out[n, PART : PART + 2, :] = jnp.broadcast_to(power, (2, 256))


def parts_body(gathered, _after, cells, taps):
    cells[...] = gathered[:, CELLS:TAPS_AT]
    taps[...] = gathered[:, TAPS_AT:WIDE]


def scaled_down(values):
    most = jnp.full((1, 256), jnp.max(jnp.abs(values)), F32)
    power = jnp.ceil(jnp.log2(jnp.maximum(most, 2.0**-100)))
    return power, values * jnp.exp2(14.0 - power)


def sum_body(factor, peers, parts, *rest):
    out = rest[-1]
    total = jnp.zeros((PART, 256), F32)
    for n in range(peers):
        total = total + parts[n, 0:PART, :] * jnp.exp2(parts[n, PART : PART + 1, :] - 14.0)
    power, scaled = scaled_down(total * factor)
    out[0:PART, :] = scaled
    out[PART : PART + 2, :] = jnp.broadcast_to(power, (2, 256))


def finish_body(full, out_far, out, sent):
    half = ROWS // 2
    copies = []
    for h in range(2):
        for n in range(4 * h, 4 * h + 4):
            scale = jnp.exp2(full[n, PART : PART + 1, :] - 14.0)
            out[PART * n : PART * n + PART, :] = full[n, 0:PART, :] * scale
        here = pl.ds(half * h, half)
        copies.append(pltpu.make_async_copy(out.at[here], out_far.at[here], sent.at[h]))
        copies[h].start()
    for copy in copies:
        copy.wait()


def far_body(own, far, out):
    out[...] = own[...] + far[...]


def outputs_body(own, near, out_field, input_grad):
    for out, at in ((out_field, 0), (input_grad, OWN)):
        for r in range(2):
            for z in range(4):
                here = (slice(at, at + OWN), slice(128 * (4 * r + z), 128 * (4 * r + z) + 128))
                out[:, r, z, :] = (own[here] + near[here]).astype(BF)


def contributions_body(core, side_at, gathered, filters, swapped, halves, near, far, mid, products):
    first, side = core[0] == 0, side_at[0]
    products[...] = jnp.dot(
        filters[...].reshape(ROWS, 256), gathered[:, 0:CELLS], preferred_element_type=F32
    )
    put(products, 1, first, 0, near, far, mid)
    mine = gathered[:, TAPS_AT:WIDE]
    other = swapped[...]
    low, high = jnp.where(first, mine, other), jnp.where(first, other, mine)
    over = (((0,), (0,)), ((), ()))
    for r in range(2):
        rows = []
        for line in range(2):
            here = slice(128 * line, 128 * line + 128)
            kept = (side == line) if r == 0 else (side != line)
            rows.append(jnp.where(kept, gathered[here, CELLS:TAPS_AT], halves[here, :]))
        cells = jnp.concatenate(rows, axis=0)
        at = slice(HALF_CELLS * r, HALF_CELLS * r + HALF_CELLS)
        products[0:256, at] = lax.dot_general(low, cells, over, preferred_element_type=F32)
        products[176:ROWS, at] = lax.dot_general(high, cells, over, preferred_element_type=F32)
    put(products, -1, first, OWN, near, far, mid)


def put(products, sign, first, at, near, far, mid):
    following, last = taps_sum(products, 1 - sign, sign), taps_sum(products, 1 + sign, sign)
    for n, block in enumerate(taps_sum(products, 1, sign)):
        here = (slice(at, at + OWN), slice(128 * n, 128 * n + 128))
        mid[here] = block
        near[here] = jnp.where(first, following[n], last[n])
        far[here] = jnp.where(first, last[n], following[n])


def per_device(field, filters, cotangent):
    space = ("far", "near", "core")
    chan = ("side", "line")
    core, side = (lax.axis_index(name).astype(jnp.int32).reshape(1) for name in ("core", "side"))
    up = [(i, i + 1) for i in range(31)]
    down = [(i + 1, i) for i in range(31)]
    swap = [(0, 1), (1, 0)]
    across = [pair for i in range(1, 31, 2) for pair in ((i, i + 1), (i + 1, i))]

    packed, own_cot = call(
        pack_body,
        [shape((16, OWN, WIDE), BF), shape((OWN, CELLS), BF)],
        [SMEM] * 2 + [FAR] * 3,
        [
            pltpu.VMEM((OWN, 2, 4, 128), BF),
            pltpu.VMEM((OWN, 2, 4, 128), BF),
            pltpu.VMEM((16, OWN, 256), BF),
            pltpu.VMEM((2, OWN, TAPS_AT), BF),
            pltpu.VMEM((16, OWN, 256), BF),
            pltpu.SemaphoreType.DMA((3,)),
            pltpu.SemaphoreType.DMA((17,)),
        ],
        moved=1 << 20,
        limit=PACK_LIMIT,
        outs_at=[FAR, VMEM],
    )(core, side, field, cotangent, filters)
    gathered = lax.all_to_all(packed, chan, 0, 0).reshape(256, WIDE)
    below = lax.ppermute(own_cot, space, up)
    above = lax.ppermute(own_cot, space, down)

    own_grad = call(
        grad_body,
        [shape((8, PART + 2, 256), F32)],
        [VMEM] * 4,
        [pltpu.VMEM((ROWS, CELLS), BF)],
        flops=2 * ROWS * CELLS * 256,
        moved=1 << 20,
    )(gathered, below, own_cot, above)[0]
    half_cells, half_taps = call(
        parts_body, [shape((256, HALF_CELLS), BF), shape((256, 256), BF)], [VMEM, ANY], moved=1 << 19
    )(gathered, own_grad)
    halves = lax.ppermute(half_cells, "side", swap)
    swapped = lax.ppermute(half_taps, "core", swap)
    parts = lax.all_to_all(own_grad.astype(HALF), ("core", "near"), 0, 0).astype(F32)
    to_near, to_far, own_sums = call(
        contributions_body,
        [shape((2 * OWN, CELLS), F32)] * 3,
        [SMEM] * 2 + [VMEM] * 4,
        [pltpu.VMEM((ROWS, CELLS), F32)],
        flops=CONTRIBUTIONS_FLOPS,
        moved=1 << 20,
    )(core, side, gathered, filters, swapped, halves)
    from_far = lax.ppermute(to_far, space, across)

    def summed(factor, peers, flops, parts, *after):
        body = functools.partial(sum_body, factor, peers)
        return call(body, [shape((PART + 2, 256), F32)], [VMEM] + [ANY] * len(after), flops=flops)(
            parts, *after
        )[0]

    def spread(part, peers, axes):
        many = jnp.broadcast_to(part.astype(HALF)[None], (peers,) + part.shape)
        return lax.all_to_all(many, axes, 0, 0).astype(F32)

    row = summed(1.0, 8, ROW_FLOPS, parts)
    mine = summed(SCALE, 4, 0, spread(row, 4, "far"), own_sums)
    from_near = lax.ppermute(to_near, "core", swap)
    full = spread(mine, 8, ("core", "near"))
    weight_grad = call(
        finish_body,
        [shape((ROWS, 256), F32)],
        [VMEM],
        [pltpu.VMEM((ROWS, 256), F32), pltpu.SemaphoreType.DMA((2,))],
        moved=1 << 20,
        outs_at=[FAR],
    )(full)[0]
    own_and_far = call(far_body, [shape((2 * OWN, CELLS), F32)], [VMEM] * 2, flops=FAR_FLOPS)(
        own_sums, from_far
    )[0]
    out_field, input_grad = call(outputs_body, [shape(field.shape, BF)] * 2, [VMEM] * 2, moved=1 << 18)(
        own_and_far, from_near
    )
    return out_field, input_grad, weight_grad.reshape(TAPS, OWN, 256)


def solution(mesh):
    fine = Mesh(mesh.devices.reshape(4, 4, 2, 2, 8), ("far", "near", "core", "side", "line"))
    cells = P(("side", "line"), ("far", "near", "core"), None, None)
    taps = P(None, ("side", "line"), None)
    return jax.shard_map(
        per_device,
        mesh=fine,
        in_specs=(cells, taps, cells),
        out_specs=(cells, cells, taps),
        check_vma=False,
    )
```

```python
import functools
import math

import jax
import jax.numpy as jnp
from jax import lax
from jax.experimental import pallas as pl
from jax.experimental.pallas import tpu as pltpu
from jax.sharding import Mesh
from jax.sharding import PartitionSpec as P

BF = jnp.bfloat16
F32 = jnp.float32
HALF = jnp.float16
ANY = pl.BlockSpec(memory_space=pl.ANY)
SMEM = pl.BlockSpec(memory_space=pltpu.SMEM)
FAR = pl.BlockSpec(memory_space=pltpu.HBM)
VMEM = pl.BlockSpec(memory_space=pltpu.VMEM)
TAPS = 27
OWN = 16
CELLS = 1024
ROWS = TAPS * OWN
HALF_CELLS = CELLS // 2
TAPS_AT = CELLS + HALF_CELLS
WIDE = TAPS_AT + 256
PART = ROWS // 8
SCALE = 1.0 / math.sqrt(32768)
LIMIT = 16 * 1024 * 1024
PACK_LIMIT = 63 * 1024 * 1024
CONTRIBUTIONS_FLOPS = 10**10
ROW_FLOPS = 10**9
FAR_FLOPS = 15 * 10**8


def call(body, outs, ins, scratch=(), flops=0, moved=0, limit=LIMIT, outs_at=None):
    return pl.pallas_call(
        body,
        out_shape=outs,
        in_specs=ins,
        out_specs=outs_at or [VMEM] * len(outs),
        scratch_shapes=list(scratch),
        compiler_params=pltpu.CompilerParams(vmem_limit_bytes=limit),
        cost_estimate=pl.CostEstimate(flops=flops, bytes_accessed=moved, transcendentals=0),
    )


def shape(dims, kind):
    return jax.ShapeDtypeStruct(dims, kind)


def lanes(dims):
    return lax.broadcasted_iota(jnp.int32, dims, len(dims) - 1)


def moved_by(block, step):
    if step == 0:
        return block
    at = lanes(block.shape) + step
    turned = pltpu.roll(block, (-step) % 128, 1)
    return jnp.where((at >= 0) & (at < 128), turned, 0.0)


def pack_body(
    core_at, side_at, field_far, cot_far, filters_far, out, own_far,
    field, cotangent, filters, own_cot, cells, taps, arrived, sent,
):
    core, side = core_at[0], side_at[0]
    own_taps = filters_far.at[pl.ds(11 * core, 16)]
    pairs = ((field_far, field), (cot_far, cotangent), (own_taps, filters))
    copies = [pltpu.make_async_copy(a, b, arrived.at[n]) for n, (a, b) in enumerate(pairs)]
    for copy in copies:
        copy.start()
    copies[0].wait()
    copies[1].wait()
    for r in range(2):
        for z in range(4):
            at = 128 * (4 * r + z)
            mine = cotangent[:, r, z, :]
            own_cot[:, at : at + 128] = mine
            cells[0, :, at : at + 128] = field[:, r, z, :]
            cells[1, :, at : at + 128] = field[:, r, z, :]
            at = CELLS + 128 * z
            cells[jnp.where(side == r, 0, 1), :, at : at + 128] = mine
    sends = [
        pltpu.make_async_copy(cells.at[c // 8], out.at[c, :, pl.ds(0, TAPS_AT)], sent.at[c])
        for c in range(16)
    ]
    sends.append(pltpu.make_async_copy(own_cot, own_far, sent.at[17]))
    for send in sends:
        send.start()
    copies[2].wait()
    lane = lanes((OWN, 128))
    for g in range(2):
        parts = [jnp.zeros((OWN, 128), F32) for _ in range(16)]
        for j in range(8):
            here = (lane >= 16 * j) & (lane < 16 * j + 16)
            tap = filters[8 * g + j].astype(F32)
            for h in range(2):
                block = tap[:, 128 * h : 128 * h + 128]
                for q in range(8):
                    step = (16 * (j - q)) % 128
                    turned = block if step == 0 else pltpu.roll(block, step, 1)
                    parts[8 * h + q] = jnp.where(here, turned, parts[8 * h + q])
        for c in range(16):
            taps[c, :, 128 * g : 128 * g + 128] = parts[c].astype(BF)
    last = pltpu.make_async_copy(taps, out.at[:, :, pl.ds(TAPS_AT, 256)], sent.at[16])
    last.start()
    for send in sends:
        send.wait()
    last.wait()


def taps_sum(products, a, sign):
    blocks = []
    for r in range(2):
        for z in range(4):
            total = None
            for c in range(3):
                column = None
                for b in range(3):
                    source = z + sign * 2 * (b - 1)
                    if source < 0 or source > 3:
                        continue
                    k = 9 * a + 3 * b + c
                    lane = 128 * (4 * r + source)
                    part = products[16 * k : 16 * k + 16, lane : lane + 128]
                    column = part if column is None else column + part
                column = moved_by(column, sign * 2 * (c - 1))
                total = column if total is None else total + column
            blocks.append(total)
    return blocks


def grad_body(gathered, below, own, above, out, shifted):
    zero = jnp.zeros((OWN, 128), BF)
    for a, source in ((0, above), (1, own), (2, below)):
        for r in range(2):
            rolled = []
            for z in range(4):
                lane = 128 * (4 * r + z)
                block = source[:, lane : lane + 128].astype(F32)
                rolled.append([moved_by(block, -2 * (c - 1)).astype(BF) for c in range(3)])
            for z in range(4):
                for b in range(3):
                    at = z - 2 * (b - 1)
                    for c in range(3):
                        k = 9 * a + 3 * b + c
                        lane = 128 * (4 * r + z)
                        shifted[16 * k : 16 * k + 16, lane : lane + 128] = (
                            rolled[at][c] if 0 <= at < 4 else zero
                        )
    total = lax.dot_general(
        shifted[...],
        gathered[:, 0:CELLS],
        (((1,), (1,)), ((), ())),
        preferred_element_type=F32,
    )
    power, scaled = scaled_down(total)
    for n in range(8):
        out[n, 0:PART, :] = scaled[PART * n : PART * n + PART, :]
        out[n, PART : PART + 2, :] = jnp.broadcast_to(power, (2, 256))


def parts_body(gathered, _after, cells, taps):
    cells[...] = gathered[:, CELLS:TAPS_AT]
    taps[...] = gathered[:, TAPS_AT:WIDE]


def scaled_down(values):
    most = jnp.full((1, 256), jnp.max(jnp.abs(values)), F32)
    power = jnp.ceil(jnp.log2(jnp.maximum(most, 2.0**-100)))
    return power, values * jnp.exp2(14.0 - power)


def sum_body(factor, peers, parts, *rest):
    out = rest[-1]
    total = jnp.zeros((PART, 256), F32)
    for n in range(peers):
        total = total + parts[n, 0:PART, :] * jnp.exp2(parts[n, PART : PART + 1, :] - 14.0)
    power, scaled = scaled_down(total * factor)
    out[0:PART, :] = scaled
    out[PART : PART + 2, :] = jnp.broadcast_to(power, (2, 256))


def finish_body(full, out_far, out, sent):
    half = ROWS // 2
    copies = []
    for h in range(2):
        for n in range(4 * h, 4 * h + 4):
            scale = jnp.exp2(full[n, PART : PART + 1, :] - 14.0)
            out[PART * n : PART * n + PART, :] = full[n, 0:PART, :] * scale
        here = pl.ds(half * h, half)
        copies.append(pltpu.make_async_copy(out.at[here], out_far.at[here], sent.at[h]))
        copies[h].start()
    for copy in copies:
        copy.wait()


def far_body(own, far, out):
    out[...] = own[...] + far[...]


def outputs_body(own, near, out_field, input_grad):
    for out, at in ((out_field, 0), (input_grad, OWN)):
        for r in range(2):
            for z in range(4):
                here = (slice(at, at + OWN), slice(128 * (4 * r + z), 128 * (4 * r + z) + 128))
                out[:, r, z, :] = (own[here] + near[here]).astype(BF)


def contributions_body(core, side_at, gathered, filters, swapped, halves, near, far, mid, products):
    first, side = core[0] == 0, side_at[0]
    products[...] = jnp.dot(
        filters[...].reshape(ROWS, 256), gathered[:, 0:CELLS], preferred_element_type=F32
    )
    put(products, 1, first, 0, near, far, mid)
    mine = gathered[:, TAPS_AT:WIDE]
    other = swapped[...]
    low, high = jnp.where(first, mine, other), jnp.where(first, other, mine)
    over = (((0,), (0,)), ((), ()))
    for r in range(2):
        rows = []
        for line in range(2):
            here = slice(128 * line, 128 * line + 128)
            kept = (side == line) if r == 0 else (side != line)
            rows.append(jnp.where(kept, gathered[here, CELLS:TAPS_AT], halves[here, :]))
        cells = jnp.concatenate(rows, axis=0)
        at = slice(HALF_CELLS * r, HALF_CELLS * r + HALF_CELLS)
        products[0:256, at] = lax.dot_general(low, cells, over, preferred_element_type=F32)
        products[176:ROWS, at] = lax.dot_general(high, cells, over, preferred_element_type=F32)
    put(products, -1, first, OWN, near, far, mid)


def put(products, sign, first, at, near, far, mid):
    following, last = taps_sum(products, 1 - sign, sign), taps_sum(products, 1 + sign, sign)
    for n, block in enumerate(taps_sum(products, 1, sign)):
        here = (slice(at, at + OWN), slice(128 * n, 128 * n + 128))
        mid[here] = block
        near[here] = jnp.where(first, following[n], last[n])
        far[here] = jnp.where(first, last[n], following[n])


def per_device(field, filters, cotangent):
    space = ("far", "near", "core")
    chan = ("side", "line")
    core, side = (lax.axis_index(name).astype(jnp.int32).reshape(1) for name in ("core", "side"))
    up = [(i, i + 1) for i in range(31)]
    down = [(i + 1, i) for i in range(31)]
    swap = [(0, 1), (1, 0)]
    across = [pair for i in range(1, 31, 2) for pair in ((i, i + 1), (i + 1, i))]

    packed, own_cot = call(
        pack_body,
        [shape((16, OWN, WIDE), BF), shape((OWN, CELLS), BF)],
        [SMEM] * 2 + [FAR] * 3,
        [
            pltpu.VMEM((OWN, 2, 4, 128), BF),
            pltpu.VMEM((OWN, 2, 4, 128), BF),
            pltpu.VMEM((16, OWN, 256), BF),
            pltpu.VMEM((OWN, CELLS), BF),
            pltpu.VMEM((2, OWN, TAPS_AT), BF),
            pltpu.VMEM((16, OWN, 256), BF),
            pltpu.SemaphoreType.DMA((3,)),
            pltpu.SemaphoreType.DMA((18,)),
        ],
        moved=1 << 20,
        limit=PACK_LIMIT,
        outs_at=[FAR, FAR],
    )(core, side, field, cotangent, filters)
    gathered = lax.all_to_all(packed, chan, 0, 0).reshape(256, WIDE)
    below = lax.ppermute(own_cot, space, up)
    above = lax.ppermute(own_cot, space, down)

    own_grad = call(
        grad_body,
        [shape((8, PART + 2, 256), F32)],
        [VMEM] * 4,
        [pltpu.VMEM((ROWS, CELLS), BF)],
        flops=2 * ROWS * CELLS * 256,
        moved=1 << 20,
    )(gathered, below, own_cot, above)[0]
    half_cells, half_taps = call(
        parts_body, [shape((256, HALF_CELLS), BF), shape((256, 256), BF)], [VMEM, ANY], moved=1 << 19
    )(gathered, own_grad)
    halves = lax.ppermute(half_cells, "side", swap)
    swapped = lax.ppermute(half_taps, "core", swap)
    parts = lax.all_to_all(own_grad.astype(HALF), ("core", "near"), 0, 0).astype(F32)
    to_near, to_far, own_sums = call(
        contributions_body,
        [shape((2 * OWN, CELLS), F32)] * 3,
        [SMEM] * 2 + [VMEM] * 4,
        [pltpu.VMEM((ROWS, CELLS), F32)],
        flops=CONTRIBUTIONS_FLOPS,
        moved=1 << 20,
    )(core, side, gathered, filters, swapped, halves)
    from_far = lax.ppermute(to_far, space, across)

    def summed(factor, peers, flops, parts, *after):
        body = functools.partial(sum_body, factor, peers)
        return call(body, [shape((PART + 2, 256), F32)], [VMEM] + [ANY] * len(after), flops=flops)(
            parts, *after
        )[0]

    def spread(part, peers, axes):
        many = jnp.broadcast_to(part.astype(HALF)[None], (peers,) + part.shape)
        return lax.all_to_all(many, axes, 0, 0).astype(F32)

    row = summed(1.0, 8, ROW_FLOPS, parts)
    mine = summed(SCALE, 4, 0, spread(row, 4, "far"), own_sums)
    from_near = lax.ppermute(to_near, "core", swap)
    full = spread(mine, 8, ("core", "near"))
    weight_grad = call(
        finish_body,
        [shape((ROWS, 256), F32)],
        [VMEM],
        [pltpu.VMEM((ROWS, 256), F32), pltpu.SemaphoreType.DMA((2,))],
        moved=1 << 20,
        outs_at=[FAR],
    )(full)[0]
    own_and_far = call(far_body, [shape((2 * OWN, CELLS), F32)], [VMEM] * 2, flops=FAR_FLOPS)(
        own_sums, from_far
    )[0]
    out_field, input_grad = call(outputs_body, [shape(field.shape, BF)] * 2, [VMEM] * 2, moved=1 << 18)(
        own_and_far, from_near
    )
    return out_field, input_grad, weight_grad.reshape(TAPS, OWN, 256)


def solution(mesh):
    fine = Mesh(mesh.devices.reshape(4, 4, 2, 2, 8), ("far", "near", "core", "side", "line"))
    cells = P(("side", "line"), ("far", "near", "core"), None, None)
    taps = P(None, ("side", "line"), None)
    return jax.shard_map(
        per_device,
        mesh=fine,
        in_specs=(cells, taps, cells),
        out_specs=(cells, cells, taps),
        check_vma=False,
    )
```

```python
import functools
import math

import jax
import jax.numpy as jnp
from jax import lax
from jax.experimental import pallas as pl
from jax.experimental.pallas import tpu as pltpu
from jax.sharding import Mesh
from jax.sharding import PartitionSpec as P

BF = jnp.bfloat16
F32 = jnp.float32
HALF = jnp.float16
ANY = pl.BlockSpec(memory_space=pl.ANY)
SMEM = pl.BlockSpec(memory_space=pltpu.SMEM)
FAR = pl.BlockSpec(memory_space=pltpu.HBM)
VMEM = pl.BlockSpec(memory_space=pltpu.VMEM)
TAPS = 27
OWN = 16
CELLS = 1024
ROWS = TAPS * OWN
HALF_CELLS = CELLS // 2
TAPS_AT = CELLS + HALF_CELLS
WIDE = TAPS_AT + 256
PART = ROWS // 8
SCALE = 1.0 / math.sqrt(32768)
LIMIT = 16 * 1024 * 1024
PACK_LIMIT = 63 * 1024 * 1024
CONTRIBUTIONS_FLOPS = 10**10
ROW_FLOPS = 10**9
FAR_FLOPS = 15 * 10**8


def call(body, outs, ins, scratch=(), flops=0, moved=0, limit=LIMIT, outs_at=None):
    return pl.pallas_call(
        body,
        out_shape=outs,
        in_specs=ins,
        out_specs=outs_at or [VMEM] * len(outs),
        scratch_shapes=list(scratch),
        compiler_params=pltpu.CompilerParams(vmem_limit_bytes=limit),
        cost_estimate=pl.CostEstimate(flops=flops, bytes_accessed=moved, transcendentals=0),
    )


def shape(dims, kind):
    return jax.ShapeDtypeStruct(dims, kind)


def lanes(dims):
    return lax.broadcasted_iota(jnp.int32, dims, len(dims) - 1)


def moved_by(block, step):
    if step == 0:
        return block
    at = lanes(block.shape) + step
    turned = pltpu.roll(block, (-step) % 128, 1)
    return jnp.where((at >= 0) & (at < 128), turned, 0.0)


def pack_body(
    core_at, side_at, field_far, cot_far, filters_far, out, own_far,
    field, cotangent, filters, own_cot, cells, taps, arrived, sent,
):
    core, side = core_at[0], side_at[0]
    own_taps = filters_far.at[pl.ds(11 * core, 16)]
    pairs = ((field_far, field), (cot_far, cotangent), (own_taps, filters))
    copies = [pltpu.make_async_copy(a, b, arrived.at[n]) for n, (a, b) in enumerate(pairs)]
    for copy in copies:
        copy.start()
    copies[0].wait()
    copies[1].wait()
    for r in range(2):
        for z in range(4):
            at = 128 * (4 * r + z)
            mine = cotangent[:, r, z, :]
            own_cot[:, at : at + 128] = mine
            cells[0, :, at : at + 128] = field[:, r, z, :]
            cells[1, :, at : at + 128] = field[:, r, z, :]
            at = CELLS + 128 * z
            cells[jnp.where(side == r, 0, 1), :, at : at + 128] = mine
    sends = [
        pltpu.make_async_copy(cells.at[c // 8], out.at[c, :, pl.ds(0, TAPS_AT)], sent.at[c])
        for c in range(16)
    ]
    sends.append(pltpu.make_async_copy(own_cot, own_far, sent.at[17]))
    for send in sends:
        send.start()
    copies[2].wait()
    lane = lanes((OWN, 128))
    for g in range(2):
        parts = [jnp.zeros((OWN, 128), F32) for _ in range(16)]
        for j in range(8):
            here = (lane >= 16 * j) & (lane < 16 * j + 16)
            tap = filters[8 * g + j].astype(F32)
            for h in range(2):
                block = tap[:, 128 * h : 128 * h + 128]
                for q in range(8):
                    step = (16 * (j - q)) % 128
                    turned = block if step == 0 else pltpu.roll(block, step, 1)
                    parts[8 * h + q] = jnp.where(here, turned, parts[8 * h + q])
        for c in range(16):
            taps[c, :, 128 * g : 128 * g + 128] = parts[c].astype(BF)
    last = pltpu.make_async_copy(taps, out.at[:, :, pl.ds(TAPS_AT, 256)], sent.at[16])
    last.start()
    for send in sends:
        send.wait()
    last.wait()


def taps_sum(products, a, sign):
    blocks = []
    for r in range(2):
        for z in range(4):
            total = None
            for c in range(3):
                column = None
                for b in range(3):
                    source = z + sign * 2 * (b - 1)
                    if source < 0 or source > 3:
                        continue
                    k = 9 * a + 3 * b + c
                    lane = 128 * (4 * r + source)
                    part = products[16 * k : 16 * k + 16, lane : lane + 128]
                    column = part if column is None else column + part
                column = moved_by(column, sign * 2 * (c - 1))
                total = column if total is None else total + column
            blocks.append(total)
    return blocks


def shift_body(below, own, above, shifted):
    zero = jnp.zeros((OWN, 128), BF)
    for a, source in ((0, above), (1, own), (2, below)):
        for r in range(2):
            rolled = []
            for z in range(4):
                lane = 128 * (4 * r + z)
                block = source[:, lane : lane + 128].astype(F32)
                rolled.append([moved_by(block, -2 * (c - 1)).astype(BF) for c in range(3)])
            for z in range(4):
                for b in range(3):
                    at = z - 2 * (b - 1)
                    for c in range(3):
                        k = 9 * a + 3 * b + c
                        lane = 128 * (4 * r + z)
                        shifted[16 * k : 16 * k + 16, lane : lane + 128] = (
                            rolled[at][c] if 0 <= at < 4 else zero
                        )


def grad_body(gathered, shifted, out):
    total = lax.dot_general(
        shifted[...],
        gathered[:, 0:CELLS],
        (((1,), (1,)), ((), ())),
        preferred_element_type=F32,
    )
    power, scaled = scaled_down(total)
    for n in range(8):
        out[n, 0:PART, :] = scaled[PART * n : PART * n + PART, :]
        out[n, PART : PART + 2, :] = jnp.broadcast_to(power, (2, 256))


def parts_body(gathered, _after, cells, taps):
    cells[...] = gathered[:, CELLS:TAPS_AT]
    taps[...] = gathered[:, TAPS_AT:WIDE]


def scaled_down(values):
    most = jnp.full((1, 256), jnp.max(jnp.abs(values)), F32)
    power = jnp.ceil(jnp.log2(jnp.maximum(most, 2.0**-100)))
    return power, values * jnp.exp2(14.0 - power)


def sum_body(factor, peers, parts, *rest):
    out = rest[-1]
    total = jnp.zeros((PART, 256), F32)
    for n in range(peers):
        total = total + parts[n, 0:PART, :] * jnp.exp2(parts[n, PART : PART + 1, :] - 14.0)
    power, scaled = scaled_down(total * factor)
    out[0:PART, :] = scaled
    out[PART : PART + 2, :] = jnp.broadcast_to(power, (2, 256))


def finish_body(full, out_far, out, sent):
    half = ROWS // 2
    copies = []
    for h in range(2):
        for n in range(4 * h, 4 * h + 4):
            scale = jnp.exp2(full[n, PART : PART + 1, :] - 14.0)
            out[PART * n : PART * n + PART, :] = full[n, 0:PART, :] * scale
        here = pl.ds(half * h, half)
        copies.append(pltpu.make_async_copy(out.at[here], out_far.at[here], sent.at[h]))
        copies[h].start()
    for copy in copies:
        copy.wait()


def far_body(own, far, out):
    out[...] = own[...] + far[...]


def outputs_body(own, near, out_field, input_grad):
    for out, at in ((out_field, 0), (input_grad, OWN)):
        for r in range(2):
            for z in range(4):
                here = (slice(at, at + OWN), slice(128 * (4 * r + z), 128 * (4 * r + z) + 128))
                out[:, r, z, :] = (own[here] + near[here]).astype(BF)


def contributions_body(core, side_at, gathered, filters, swapped, halves, near, far, mid, products):
    first, side = core[0] == 0, side_at[0]
    products[...] = jnp.dot(
        filters[...].reshape(ROWS, 256), gathered[:, 0:CELLS], preferred_element_type=F32
    )
    put(products, 1, first, 0, near, far, mid)
    mine = gathered[:, TAPS_AT:WIDE]
    other = swapped[...]
    low, high = jnp.where(first, mine, other), jnp.where(first, other, mine)
    over = (((0,), (0,)), ((), ()))
    for r in range(2):
        rows = []
        for line in range(2):
            here = slice(128 * line, 128 * line + 128)
            kept = (side == line) if r == 0 else (side != line)
            rows.append(jnp.where(kept, gathered[here, CELLS:TAPS_AT], halves[here, :]))
        cells = jnp.concatenate(rows, axis=0)
        at = slice(HALF_CELLS * r, HALF_CELLS * r + HALF_CELLS)
        products[0:256, at] = lax.dot_general(low, cells, over, preferred_element_type=F32)
        products[176:ROWS, at] = lax.dot_general(high, cells, over, preferred_element_type=F32)
    put(products, -1, first, OWN, near, far, mid)


def put(products, sign, first, at, near, far, mid):
    following, last = taps_sum(products, 1 - sign, sign), taps_sum(products, 1 + sign, sign)
    for n, block in enumerate(taps_sum(products, 1, sign)):
        here = (slice(at, at + OWN), slice(128 * n, 128 * n + 128))
        mid[here] = block
        near[here] = jnp.where(first, following[n], last[n])
        far[here] = jnp.where(first, last[n], following[n])


def per_device(field, filters, cotangent):
    space = ("far", "near", "core")
    chan = ("side", "line")
    core, side = (lax.axis_index(name).astype(jnp.int32).reshape(1) for name in ("core", "side"))
    up = [(i, i + 1) for i in range(31)]
    down = [(i + 1, i) for i in range(31)]
    swap = [(0, 1), (1, 0)]
    across = [pair for i in range(1, 31, 2) for pair in ((i, i + 1), (i + 1, i))]

    packed, own_cot = call(
        pack_body,
        [shape((16, OWN, WIDE), BF), shape((OWN, CELLS), BF)],
        [SMEM] * 2 + [FAR] * 3,
        [
            pltpu.VMEM((OWN, 2, 4, 128), BF),
            pltpu.VMEM((OWN, 2, 4, 128), BF),
            pltpu.VMEM((16, OWN, 256), BF),
            pltpu.VMEM((OWN, CELLS), BF),
            pltpu.VMEM((2, OWN, TAPS_AT), BF),
            pltpu.VMEM((16, OWN, 256), BF),
            pltpu.SemaphoreType.DMA((3,)),
            pltpu.SemaphoreType.DMA((18,)),
        ],
        moved=1 << 20,
        limit=PACK_LIMIT,
        outs_at=[FAR, FAR],
    )(core, side, field, cotangent, filters)
    gathered = lax.all_to_all(packed, chan, 0, 0).reshape(256, WIDE)
    below = lax.ppermute(own_cot, space, up)
    above = lax.ppermute(own_cot, space, down)

    shifted = call(shift_body, [shape((ROWS, CELLS), BF)], [VMEM] * 3, moved=1 << 20)(
        below, own_cot, above
    )[0]
    own_grad = call(
        grad_body,
        [shape((8, PART + 2, 256), F32)],
        [VMEM] * 2,
        flops=2 * ROWS * CELLS * 256,
        moved=1 << 20,
    )(gathered, shifted)[0]
    half_cells, half_taps = call(
        parts_body, [shape((256, HALF_CELLS), BF), shape((256, 256), BF)], [VMEM, ANY], moved=1 << 19
    )(gathered, own_grad)
    halves = lax.ppermute(half_cells, "side", swap)
    swapped = lax.ppermute(half_taps, "core", swap)
    parts = lax.all_to_all(own_grad.astype(HALF), ("core", "near"), 0, 0).astype(F32)
    to_near, to_far, own_sums = call(
        contributions_body,
        [shape((2 * OWN, CELLS), F32)] * 3,
        [SMEM] * 2 + [VMEM] * 4,
        [pltpu.VMEM((ROWS, CELLS), F32)],
        flops=CONTRIBUTIONS_FLOPS,
        moved=1 << 20,
    )(core, side, gathered, filters, swapped, halves)
    from_far = lax.ppermute(to_far, space, across)

    def summed(factor, peers, flops, parts, *after):
        body = functools.partial(sum_body, factor, peers)
        return call(body, [shape((PART + 2, 256), F32)], [VMEM] + [ANY] * len(after), flops=flops)(
            parts, *after
        )[0]

    def spread(part, peers, axes):
        many = jnp.broadcast_to(part.astype(HALF)[None], (peers,) + part.shape)
        return lax.all_to_all(many, axes, 0, 0).astype(F32)

    row = summed(1.0, 8, ROW_FLOPS, parts)
    mine = summed(SCALE, 4, 0, spread(row, 4, "far"), own_sums)
    from_near = lax.ppermute(to_near, "core", swap)
    full = spread(mine, 8, ("core", "near"))
    weight_grad = call(
        finish_body,
        [shape((ROWS, 256), F32)],
        [VMEM],
        [pltpu.VMEM((ROWS, 256), F32), pltpu.SemaphoreType.DMA((2,))],
        moved=1 << 20,
        outs_at=[FAR],
    )(full)[0]
    own_and_far = call(far_body, [shape((2 * OWN, CELLS), F32)], [VMEM] * 2, flops=FAR_FLOPS)(
        own_sums, from_far
    )[0]
    out_field, input_grad = call(outputs_body, [shape(field.shape, BF)] * 2, [VMEM] * 2, moved=1 << 18)(
        own_and_far, from_near
    )
    return out_field, input_grad, weight_grad.reshape(TAPS, OWN, 256)


def solution(mesh):
    fine = Mesh(mesh.devices.reshape(4, 4, 2, 2, 8), ("far", "near", "core", "side", "line"))
    cells = P(("side", "line"), ("far", "near", "core"), None, None)
    taps = P(None, ("side", "line"), None)
    return jax.shard_map(
        per_device,
        mesh=fine,
        in_specs=(cells, taps, cells),
        out_specs=(cells, cells, taps),
        check_vma=False,
    )
```

```python
import functools
import math

import jax
import jax.numpy as jnp
from jax import lax
from jax.experimental import pallas as pl
from jax.experimental.pallas import tpu as pltpu
from jax.sharding import Mesh
from jax.sharding import PartitionSpec as P

BF = jnp.bfloat16
F32 = jnp.float32
HALF = jnp.float16
ANY = pl.BlockSpec(memory_space=pl.ANY)
SMEM = pl.BlockSpec(memory_space=pltpu.SMEM)
FAR = pl.BlockSpec(memory_space=pltpu.HBM)
VMEM = pl.BlockSpec(memory_space=pltpu.VMEM)
TAPS = 27
OWN = 16
CELLS = 1024
ROWS = TAPS * OWN
HALF_CELLS = CELLS // 2
TAPS_AT = CELLS + HALF_CELLS
WIDE = TAPS_AT + 256
PART = ROWS // 8
SCALE = 1.0 / math.sqrt(32768)
LIMIT = 16 * 1024 * 1024
PACK_LIMIT = 63 * 1024 * 1024
CONTRIBUTIONS_FLOPS = 10**10
ROW_FLOPS = 10**9
FAR_FLOPS = 15 * 10**8


def call(body, outs, ins, scratch=(), flops=0, moved=0, limit=LIMIT, outs_at=None):
    return pl.pallas_call(
        body,
        out_shape=outs,
        in_specs=ins,
        out_specs=outs_at or [VMEM] * len(outs),
        scratch_shapes=list(scratch),
        compiler_params=pltpu.CompilerParams(vmem_limit_bytes=limit),
        cost_estimate=pl.CostEstimate(flops=flops, bytes_accessed=moved, transcendentals=0),
    )


def shape(dims, kind):
    return jax.ShapeDtypeStruct(dims, kind)


def lanes(dims):
    return lax.broadcasted_iota(jnp.int32, dims, len(dims) - 1)


def moved_by(block, step):
    if step == 0:
        return block
    at = lanes(block.shape) + step
    turned = pltpu.roll(block, (-step) % 128, 1)
    return jnp.where((at >= 0) & (at < 128), turned, 0.0)


def pack_body(
    core_at, side_at, field_far, cot_far, filters_far, out, own_far,
    field, cotangent, filters, own_cot, cells, taps, arrived, sent,
):
    core, side = core_at[0], side_at[0]
    own_taps = filters_far.at[pl.ds(11 * core, 16)]
    pairs = ((field_far, field), (cot_far, cotangent), (own_taps, filters))
    copies = [pltpu.make_async_copy(a, b, arrived.at[n]) for n, (a, b) in enumerate(pairs)]
    for copy in copies:
        copy.start()
    copies[0].wait()
    copies[1].wait()
    for r in range(2):
        for z in range(4):
            at = 128 * (4 * r + z)
            mine = cotangent[:, r, z, :]
            own_cot[:, at : at + 128] = mine
            cells[0, :, at : at + 128] = field[:, r, z, :]
            cells[1, :, at : at + 128] = field[:, r, z, :]
            at = CELLS + 128 * z
            cells[jnp.where(side == r, 0, 1), :, at : at + 128] = mine
    sends = [
        pltpu.make_async_copy(cells.at[c // 8], out.at[c, :, pl.ds(0, TAPS_AT)], sent.at[c])
        for c in range(16)
    ]
    sends.append(pltpu.make_async_copy(own_cot, own_far, sent.at[17]))
    for send in sends:
        send.start()
    copies[2].wait()
    lane = lanes((OWN, 128))
    for g in range(2):
        parts = [jnp.zeros((OWN, 128), F32) for _ in range(16)]
        for j in range(8):
            here = (lane >= 16 * j) & (lane < 16 * j + 16)
            tap = filters[8 * g + j].astype(F32)
            for h in range(2):
                block = tap[:, 128 * h : 128 * h + 128]
                for q in range(8):
                    step = (16 * (j - q)) % 128
                    turned = block if step == 0 else pltpu.roll(block, step, 1)
                    parts[8 * h + q] = jnp.where(here, turned, parts[8 * h + q])
        for c in range(16):
            taps[c, :, 128 * g : 128 * g + 128] = parts[c].astype(BF)
    last = pltpu.make_async_copy(taps, out.at[:, :, pl.ds(TAPS_AT, 256)], sent.at[16])
    last.start()
    for send in sends:
        send.wait()
    last.wait()


def taps_sum(products, a, sign):
    blocks = []
    for r in range(2):
        for z in range(4):
            total = None
            for c in range(3):
                column = None
                for b in range(3):
                    source = z + sign * 2 * (b - 1)
                    if source < 0 or source > 3:
                        continue
                    k = 9 * a + 3 * b + c
                    lane = 128 * (4 * r + source)
                    part = products[16 * k : 16 * k + 16, lane : lane + 128]
                    column = part if column is None else column + part
                column = moved_by(column, sign * 2 * (c - 1))
                total = column if total is None else total + column
            blocks.append(total)
    return blocks


def shift_body(below, own, above, shifted):
    zero = jnp.zeros((OWN, 128), BF)
    for a, source in ((0, above), (1, own), (2, below)):
        for r in range(2):
            rolled = []
            for z in range(4):
                lane = 128 * (4 * r + z)
                block = source[:, lane : lane + 128].astype(F32)
                rolled.append([moved_by(block, -2 * (c - 1)).astype(BF) for c in range(3)])
            for z in range(4):
                for b in range(3):
                    at = z - 2 * (b - 1)
                    for c in range(3):
                        k = 9 * a + 3 * b + c
                        lane = 128 * (4 * r + z)
                        shifted[16 * k : 16 * k + 16, lane : lane + 128] = (
                            rolled[at][c] if 0 <= at < 4 else zero
                        )


def grad_body(gathered, shifted, out):
    total = lax.dot_general(
        shifted[...],
        gathered[:, 0:CELLS],
        (((1,), (1,)), ((), ())),
        preferred_element_type=F32,
    )
    power, scaled = scaled_down(total)
    for n in range(8):
        out[n, 0:PART, :] = scaled[PART * n : PART * n + PART, :]
        out[n, PART : PART + 2, :] = jnp.broadcast_to(power, (2, 256))


def parts_body(gathered, _after, cells, taps):
    cells[...] = gathered[:, CELLS:TAPS_AT]
    taps[...] = gathered[:, TAPS_AT:WIDE]


def scaled_down(values):
    most = jnp.full((1, 256), jnp.max(jnp.abs(values)), F32)
    power = jnp.ceil(jnp.log2(jnp.maximum(most, 2.0**-100)))
    return power, values * jnp.exp2(14.0 - power)


def sum_body(factor, peers, parts, *rest):
    out = rest[-1]
    total = jnp.zeros((PART, 256), F32)
    for n in range(peers):
        total = total + parts[n, 0:PART, :] * jnp.exp2(parts[n, PART : PART + 1, :] - 14.0)
    power, scaled = scaled_down(total * factor)
    for n in range(out.shape[0]):
        out[n, 0:PART, :] = scaled
        out[n, PART : PART + 2, :] = jnp.broadcast_to(power, (2, 256))


def finish_body(full, out_far, out, sent):
    half = ROWS // 2
    copies = []
    for h in range(2):
        for n in range(4 * h, 4 * h + 4):
            scale = jnp.exp2(full[n, PART : PART + 1, :] - 14.0)
            out[PART * n : PART * n + PART, :] = full[n, 0:PART, :] * scale
        here = pl.ds(half * h, half)
        copies.append(pltpu.make_async_copy(out.at[here], out_far.at[here], sent.at[h]))
        copies[h].start()
    for copy in copies:
        copy.wait()


def far_body(own, far, out):
    out[...] = own[...] + far[...]


def outputs_body(own, near, out_field, input_grad):
    for out, at in ((out_field, 0), (input_grad, OWN)):
        for r in range(2):
            for z in range(4):
                here = (slice(at, at + OWN), slice(128 * (4 * r + z), 128 * (4 * r + z) + 128))
                out[:, r, z, :] = (own[here] + near[here]).astype(BF)


def contributions_body(core, side_at, gathered, filters, swapped, halves, near, far, mid, products):
    first, side = core[0] == 0, side_at[0]
    products[...] = jnp.dot(
        filters[...].reshape(ROWS, 256), gathered[:, 0:CELLS], preferred_element_type=F32
    )
    put(products, 1, first, 0, near, far, mid)
    mine = gathered[:, TAPS_AT:WIDE]
    other = swapped[...]
    low, high = jnp.where(first, mine, other), jnp.where(first, other, mine)
    over = (((0,), (0,)), ((), ()))
    for r in range(2):
        rows = []
        for line in range(2):
            here = slice(128 * line, 128 * line + 128)
            kept = (side == line) if r == 0 else (side != line)
            rows.append(jnp.where(kept, gathered[here, CELLS:TAPS_AT], halves[here, :]))
        cells = jnp.concatenate(rows, axis=0)
        at = slice(HALF_CELLS * r, HALF_CELLS * r + HALF_CELLS)
        products[0:256, at] = lax.dot_general(low, cells, over, preferred_element_type=F32)
        products[176:ROWS, at] = lax.dot_general(high, cells, over, preferred_element_type=F32)
    put(products, -1, first, OWN, near, far, mid)


def put(products, sign, first, at, near, far, mid):
    following, last = taps_sum(products, 1 - sign, sign), taps_sum(products, 1 + sign, sign)
    for n, block in enumerate(taps_sum(products, 1, sign)):
        here = (slice(at, at + OWN), slice(128 * n, 128 * n + 128))
        mid[here] = block
        near[here] = jnp.where(first, following[n], last[n])
        far[here] = jnp.where(first, last[n], following[n])


def per_device(field, filters, cotangent):
    space = ("far", "near", "core")
    chan = ("side", "line")
    core, side = (lax.axis_index(name).astype(jnp.int32).reshape(1) for name in ("core", "side"))
    up = [(i, i + 1) for i in range(31)]
    down = [(i + 1, i) for i in range(31)]
    swap = [(0, 1), (1, 0)]
    across = [pair for i in range(1, 31, 2) for pair in ((i, i + 1), (i + 1, i))]

    packed, own_cot = call(
        pack_body,
        [shape((16, OWN, WIDE), BF), shape((OWN, CELLS), BF)],
        [SMEM] * 2 + [FAR] * 3,
        [
            pltpu.VMEM((OWN, 2, 4, 128), BF),
            pltpu.VMEM((OWN, 2, 4, 128), BF),
            pltpu.VMEM((16, OWN, 256), BF),
            pltpu.VMEM((OWN, CELLS), BF),
            pltpu.VMEM((2, OWN, TAPS_AT), BF),
            pltpu.VMEM((16, OWN, 256), BF),
            pltpu.SemaphoreType.DMA((3,)),
            pltpu.SemaphoreType.DMA((18,)),
        ],
        moved=1 << 20,
        limit=PACK_LIMIT,
        outs_at=[FAR, FAR],
    )(core, side, field, cotangent, filters)
    gathered = lax.all_to_all(packed, chan, 0, 0).reshape(256, WIDE)
    below = lax.ppermute(own_cot, space, up)
    above = lax.ppermute(own_cot, space, down)

    shifted = call(shift_body, [shape((ROWS, CELLS), BF)], [VMEM] * 3, moved=1 << 20)(
        below, own_cot, above
    )[0]
    own_grad = call(
        grad_body,
        [shape((8, PART + 2, 256), F32)],
        [VMEM] * 2,
        flops=2 * ROWS * CELLS * 256,
        moved=1 << 20,
    )(gathered, shifted)[0]
    half_cells, half_taps = call(
        parts_body, [shape((256, HALF_CELLS), BF), shape((256, 256), BF)], [VMEM, ANY], moved=1 << 19
    )(gathered, own_grad)
    halves = lax.ppermute(half_cells, "side", swap)
    swapped = lax.ppermute(half_taps, "core", swap)
    parts = lax.all_to_all(own_grad.astype(HALF), ("core", "near"), 0, 0).astype(F32)
    to_near, to_far, own_sums = call(
        contributions_body,
        [shape((2 * OWN, CELLS), F32)] * 3,
        [SMEM] * 2 + [VMEM] * 4,
        [pltpu.VMEM((ROWS, CELLS), F32)],
        flops=CONTRIBUTIONS_FLOPS,
        moved=1 << 20,
    )(core, side, gathered, filters, swapped, halves)
    from_far = lax.ppermute(to_far, space, across)

    def summed(factor, peers, following, flops, parts, *after):
        body = functools.partial(sum_body, factor, peers)
        outs = [shape((following, PART + 2, 256), F32)]
        return call(body, outs, [VMEM] + [ANY] * len(after), flops=flops)(parts, *after)[0]

    def spread(many, axes):
        return lax.all_to_all(many.astype(HALF), axes, 0, 0).astype(F32)

    row = summed(1.0, 8, 4, ROW_FLOPS, parts)
    mine = summed(SCALE, 4, 8, 0, spread(row, "far"), own_sums)
    from_near = lax.ppermute(to_near, "core", swap)
    full = spread(mine, ("core", "near"))
    weight_grad = call(
        finish_body,
        [shape((ROWS, 256), F32)],
        [VMEM],
        [pltpu.VMEM((ROWS, 256), F32), pltpu.SemaphoreType.DMA((2,))],
        moved=1 << 20,
        outs_at=[FAR],
    )(full)[0]
    own_and_far = call(far_body, [shape((2 * OWN, CELLS), F32)], [VMEM] * 2, flops=FAR_FLOPS)(
        own_sums, from_far
    )[0]
    out_field, input_grad = call(outputs_body, [shape(field.shape, BF)] * 2, [VMEM] * 2, moved=1 << 18)(
        own_and_far, from_near
    )
    return out_field, input_grad, weight_grad.reshape(TAPS, OWN, 256)


def solution(mesh):
    fine = Mesh(mesh.devices.reshape(4, 4, 2, 2, 8), ("far", "near", "core", "side", "line"))
    cells = P(("side", "line"), ("far", "near", "core"), None, None)
    taps = P(None, ("side", "line"), None)
    return jax.shard_map(
        per_device,
        mesh=fine,
        in_specs=(cells, taps, cells),
        out_specs=(cells, cells, taps),
        check_vma=False,
    )
```

```python
import functools
import math

import jax
import jax.numpy as jnp
from jax import lax
from jax.experimental import pallas as pl
from jax.experimental.pallas import tpu as pltpu
from jax.sharding import Mesh
from jax.sharding import PartitionSpec as P

BF = jnp.bfloat16
F32 = jnp.float32
HALF = jnp.float16
ANY = pl.BlockSpec(memory_space=pl.ANY)
SMEM = pl.BlockSpec(memory_space=pltpu.SMEM)
FAR = pl.BlockSpec(memory_space=pltpu.HBM)
VMEM = pl.BlockSpec(memory_space=pltpu.VMEM)
TAPS = 27
OWN = 16
CELLS = 1024
ROWS = TAPS * OWN
HALF_CELLS = CELLS // 2
TAPS_AT = CELLS + HALF_CELLS
WIDE = TAPS_AT + 256
PART = ROWS // 8
SCALE = 1.0 / math.sqrt(32768)
LIMIT = 16 * 1024 * 1024
PACK_LIMIT = 63 * 1024 * 1024
CONTRIBUTIONS_FLOPS = 10**10
ROW_FLOPS = 10**9
FAR_FLOPS = 15 * 10**8


def call(body, outs, ins, scratch=(), flops=0, moved=0, limit=LIMIT, outs_at=None):
    return pl.pallas_call(
        body,
        out_shape=outs,
        in_specs=ins,
        out_specs=outs_at or [VMEM] * len(outs),
        scratch_shapes=list(scratch),
        compiler_params=pltpu.CompilerParams(vmem_limit_bytes=limit),
        cost_estimate=pl.CostEstimate(flops=flops, bytes_accessed=moved, transcendentals=0),
    )


def shape(dims, kind):
    return jax.ShapeDtypeStruct(dims, kind)


def lanes(dims):
    return lax.broadcasted_iota(jnp.int32, dims, len(dims) - 1)


def moved_by(block, step):
    if step == 0:
        return block
    at = lanes(block.shape) + step
    turned = pltpu.roll(block, (-step) % 128, 1)
    return jnp.where((at >= 0) & (at < 128), turned, 0.0)


def pack_body(
    core_at, side_at, field_far, cot_far, filters_far, out, own_far,
    field, cotangent, filters, own_cot, cells, taps, arrived, sent,
):
    core, side = core_at[0], side_at[0]
    own_taps = filters_far.at[pl.ds(11 * core, 16)]
    pairs = ((field_far, field), (cot_far, cotangent), (own_taps, filters))
    copies = [pltpu.make_async_copy(a, b, arrived.at[n]) for n, (a, b) in enumerate(pairs)]
    for copy in copies:
        copy.start()
    copies[0].wait()
    copies[1].wait()
    for r in range(2):
        for z in range(4):
            at = 128 * (4 * r + z)
            mine = cotangent[:, r, z, :]
            own_cot[:, at : at + 128] = mine
            cells[0, :, at : at + 128] = field[:, r, z, :]
            cells[1, :, at : at + 128] = field[:, r, z, :]
            at = CELLS + 128 * z
            cells[jnp.where(side == r, 0, 1), :, at : at + 128] = mine
    sends = [
        pltpu.make_async_copy(cells.at[c // 8], out.at[c, :, pl.ds(0, TAPS_AT)], sent.at[c])
        for c in range(16)
    ]
    sends.append(pltpu.make_async_copy(own_cot, own_far, sent.at[17]))
    for send in sends:
        send.start()
    copies[2].wait()
    lane = lanes((OWN, 128))
    for g in range(2):
        parts = [jnp.zeros((OWN, 128), F32) for _ in range(16)]
        for j in range(8):
            here = (lane >= 16 * j) & (lane < 16 * j + 16)
            tap = filters[8 * g + j].astype(F32)
            for h in range(2):
                block = tap[:, 128 * h : 128 * h + 128]
                for q in range(8):
                    step = (16 * (j - q)) % 128
                    turned = block if step == 0 else pltpu.roll(block, step, 1)
                    parts[8 * h + q] = jnp.where(here, turned, parts[8 * h + q])
        for c in range(16):
            taps[g, c] = parts[c].astype(BF)
        there = out.at[:, :, pl.ds(TAPS_AT + 128 * g, 128)]
        sends.append(pltpu.make_async_copy(taps.at[g], there, sent.at[18 if g else 16]))
        sends[-1].start()
    for send in sends:
        send.wait()


def taps_sum(products, a, sign):
    blocks = []
    for r in range(2):
        for z in range(4):
            total = None
            for c in range(3):
                column = None
                for b in range(3):
                    source = z + sign * 2 * (b - 1)
                    if source < 0 or source > 3:
                        continue
                    k = 9 * a + 3 * b + c
                    lane = 128 * (4 * r + source)
                    part = products[16 * k : 16 * k + 16, lane : lane + 128]
                    column = part if column is None else column + part
                column = moved_by(column, sign * 2 * (c - 1))
                total = column if total is None else total + column
            blocks.append(total)
    return blocks


def shift_body(below, own, above, shifted):
    zero = jnp.zeros((OWN, 128), BF)
    for a, source in ((0, above), (1, own), (2, below)):
        for r in range(2):
            rolled = []
            for z in range(4):
                lane = 128 * (4 * r + z)
                block = source[:, lane : lane + 128].astype(F32)
                rolled.append([moved_by(block, -2 * (c - 1)).astype(BF) for c in range(3)])
            for z in range(4):
                for b in range(3):
                    at = z - 2 * (b - 1)
                    for c in range(3):
                        k = 9 * a + 3 * b + c
                        lane = 128 * (4 * r + z)
                        shifted[16 * k : 16 * k + 16, lane : lane + 128] = (
                            rolled[at][c] if 0 <= at < 4 else zero
                        )


def grad_body(gathered, shifted, out):
    total = lax.dot_general(
        shifted[...],
        gathered[:, 0:CELLS],
        (((1,), (1,)), ((), ())),
        preferred_element_type=F32,
    )
    power, scaled = scaled_down(total)
    for n in range(8):
        out[n, 0:PART, :] = scaled[PART * n : PART * n + PART, :]
        out[n, PART : PART + 2, :] = jnp.broadcast_to(power, (2, 256))


def parts_body(gathered, _after, cells, taps):
    cells[...] = gathered[:, CELLS:TAPS_AT]
    taps[...] = gathered[:, TAPS_AT:WIDE]


def scaled_down(values):
    most = jnp.full((1, 256), jnp.max(jnp.abs(values)), F32)
    power = jnp.ceil(jnp.log2(jnp.maximum(most, 2.0**-100)))
    return power, values * jnp.exp2(14.0 - power)


def sum_body(factor, peers, parts, *rest):
    out = rest[-1]
    total = jnp.zeros((PART, 256), F32)
    for n in range(peers):
        total = total + parts[n, 0:PART, :] * jnp.exp2(parts[n, PART : PART + 1, :] - 14.0)
    power, scaled = scaled_down(total * factor)
    out[0:PART, :] = scaled
    out[PART : PART + 2, :] = jnp.broadcast_to(power, (2, 256))


def finish_body(full, out_far, out, sent):
    half = ROWS // 2
    copies = []
    for h in range(2):
        for n in range(4 * h, 4 * h + 4):
            scale = jnp.exp2(full[n, PART : PART + 1, :] - 14.0)
            out[PART * n : PART * n + PART, :] = full[n, 0:PART, :] * scale
        here = pl.ds(half * h, half)
        copies.append(pltpu.make_async_copy(out.at[here], out_far.at[here], sent.at[h]))
        copies[h].start()
    for copy in copies:
        copy.wait()


def far_body(own, far, out):
    out[...] = own[...] + far[...]


def outputs_body(own, near, out_field, input_grad):
    for out, at in ((out_field, 0), (input_grad, OWN)):
        for r in range(2):
            for z in range(4):
                here = (slice(at, at + OWN), slice(128 * (4 * r + z), 128 * (4 * r + z) + 128))
                out[:, r, z, :] = (own[here] + near[here]).astype(BF)


def contributions_body(core, side_at, gathered, filters, swapped, halves, near, far, mid, products):
    first, side = core[0] == 0, side_at[0]
    products[...] = jnp.dot(
        filters[...].reshape(ROWS, 256), gathered[:, 0:CELLS], preferred_element_type=F32
    )
    put(products, 1, first, 0, near, far, mid)
    mine = gathered[:, TAPS_AT:WIDE]
    other = swapped[...]
    low, high = jnp.where(first, mine, other), jnp.where(first, other, mine)
    over = (((0,), (0,)), ((), ()))
    for r in range(2):
        rows = []
        for line in range(2):
            here = slice(128 * line, 128 * line + 128)
            kept = (side == line) if r == 0 else (side != line)
            rows.append(jnp.where(kept, gathered[here, CELLS:TAPS_AT], halves[here, :]))
        cells = jnp.concatenate(rows, axis=0)
        at = slice(HALF_CELLS * r, HALF_CELLS * r + HALF_CELLS)
        products[0:256, at] = lax.dot_general(low, cells, over, preferred_element_type=F32)
        products[176:ROWS, at] = lax.dot_general(high, cells, over, preferred_element_type=F32)
    put(products, -1, first, OWN, near, far, mid)


def put(products, sign, first, at, near, far, mid):
    following, last = taps_sum(products, 1 - sign, sign), taps_sum(products, 1 + sign, sign)
    for n, block in enumerate(taps_sum(products, 1, sign)):
        here = (slice(at, at + OWN), slice(128 * n, 128 * n + 128))
        mid[here] = block
        near[here] = jnp.where(first, following[n], last[n])
        far[here] = jnp.where(first, last[n], following[n])


def per_device(field, filters, cotangent):
    space = ("far", "near", "core")
    chan = ("side", "line")
    core, side = (lax.axis_index(name).astype(jnp.int32).reshape(1) for name in ("core", "side"))
    up = [(i, i + 1) for i in range(31)]
    down = [(i + 1, i) for i in range(31)]
    swap = [(0, 1), (1, 0)]
    across = [pair for i in range(1, 31, 2) for pair in ((i, i + 1), (i + 1, i))]

    packed, own_cot = call(
        pack_body,
        [shape((16, OWN, WIDE), BF), shape((OWN, CELLS), BF)],
        [SMEM] * 2 + [FAR] * 3,
        [
            pltpu.VMEM((OWN, 2, 4, 128), BF),
            pltpu.VMEM((OWN, 2, 4, 128), BF),
            pltpu.VMEM((16, OWN, 256), BF),
            pltpu.VMEM((OWN, CELLS), BF),
            pltpu.VMEM((2, OWN, TAPS_AT), BF),
            pltpu.VMEM((2, 16, OWN, 128), BF),
            pltpu.SemaphoreType.DMA((3,)),
            pltpu.SemaphoreType.DMA((19,)),
        ],
        moved=1 << 20,
        limit=PACK_LIMIT,
        outs_at=[FAR, FAR],
    )(core, side, field, cotangent, filters)
    gathered = lax.all_to_all(packed, chan, 0, 0).reshape(256, WIDE)
    below = lax.ppermute(own_cot, space, up)
    above = lax.ppermute(own_cot, space, down)

    shifted = call(shift_body, [shape((ROWS, CELLS), BF)], [VMEM] * 3, moved=1 << 20)(
        below, own_cot, above
    )[0]
    own_grad = call(
        grad_body,
        [shape((8, PART + 2, 256), F32)],
        [VMEM] * 2,
        flops=2 * ROWS * CELLS * 256,
        moved=1 << 20,
    )(gathered, shifted)[0]
    half_cells, half_taps = call(
        parts_body, [shape((256, HALF_CELLS), BF), shape((256, 256), BF)], [VMEM, ANY], moved=1 << 19
    )(gathered, own_grad)
    halves = lax.ppermute(half_cells, "side", swap)
    swapped = lax.ppermute(half_taps, "core", swap)
    parts = lax.all_to_all(own_grad.astype(HALF), ("core", "near"), 0, 0).astype(F32)
    to_near, to_far, own_sums = call(
        contributions_body,
        [shape((2 * OWN, CELLS), F32)] * 3,
        [SMEM] * 2 + [VMEM] * 4,
        [pltpu.VMEM((ROWS, CELLS), F32)],
        flops=CONTRIBUTIONS_FLOPS,
        moved=1 << 20,
    )(core, side, gathered, filters, swapped, halves)
    from_far = lax.ppermute(to_far, space, across)

    def summed(factor, peers, flops, parts, *after):
        body = functools.partial(sum_body, factor, peers)
        return call(body, [shape((PART + 2, 256), F32)], [VMEM] + [ANY] * len(after), flops=flops)(
            parts, *after
        )[0]

    def spread(part, peers, axes):
        many = jnp.broadcast_to(part.astype(HALF)[None], (peers,) + part.shape)
        return lax.all_to_all(many, axes, 0, 0).astype(F32)

    row = summed(1.0, 8, ROW_FLOPS, parts)
    mine = summed(SCALE, 4, 0, spread(row, 4, "far"), own_sums)
    from_near = lax.ppermute(to_near, "core", swap)
    full = spread(mine, 8, ("core", "near"))
    weight_grad = call(
        finish_body,
        [shape((ROWS, 256), F32)],
        [VMEM],
        [pltpu.VMEM((ROWS, 256), F32), pltpu.SemaphoreType.DMA((2,))],
        moved=1 << 20,
        outs_at=[FAR],
    )(full)[0]
    own_and_far = call(far_body, [shape((2 * OWN, CELLS), F32)], [VMEM] * 2, flops=FAR_FLOPS)(
        own_sums, from_far
    )[0]
    out_field, input_grad = call(outputs_body, [shape(field.shape, BF)] * 2, [VMEM] * 2, moved=1 << 18)(
        own_and_far, from_near
    )
    return out_field, input_grad, weight_grad.reshape(TAPS, OWN, 256)


def solution(mesh):
    fine = Mesh(mesh.devices.reshape(4, 4, 2, 2, 8), ("far", "near", "core", "side", "line"))
    cells = P(("side", "line"), ("far", "near", "core"), None, None)
    taps = P(None, ("side", "line"), None)
    return jax.shard_map(
        per_device,
        mesh=fine,
        in_specs=(cells, taps, cells),
        out_specs=(cells, cells, taps),
        check_vma=False,
    )
```

```python
import functools
import math

import jax
import jax.numpy as jnp
from jax import lax
from jax.experimental import pallas as pl
from jax.experimental.pallas import tpu as pltpu
from jax.sharding import Mesh
from jax.sharding import PartitionSpec as P

BF = jnp.bfloat16
F32 = jnp.float32
HALF = jnp.float16
ANY = pl.BlockSpec(memory_space=pl.ANY)
SMEM = pl.BlockSpec(memory_space=pltpu.SMEM)
FAR = pl.BlockSpec(memory_space=pltpu.HBM)
VMEM = pl.BlockSpec(memory_space=pltpu.VMEM)
TAPS = 27
OWN = 16
CELLS = 1024
ROWS = TAPS * OWN
HALF_CELLS = CELLS // 2
TAPS_AT = CELLS + HALF_CELLS
WIDE = TAPS_AT + 256
PART = ROWS // 8
SCALE = 1.0 / math.sqrt(32768)
LIMIT = 16 * 1024 * 1024
PACK_LIMIT = 63 * 1024 * 1024
CONTRIBUTIONS_FLOPS = 10**10
ROW_FLOPS = 10**9
FAR_FLOPS = 15 * 10**8


def call(body, outs, ins, scratch=(), flops=0, moved=0, limit=LIMIT, outs_at=None):
    return pl.pallas_call(
        body,
        out_shape=outs,
        in_specs=ins,
        out_specs=outs_at or [VMEM] * len(outs),
        scratch_shapes=list(scratch),
        compiler_params=pltpu.CompilerParams(vmem_limit_bytes=limit),
        cost_estimate=pl.CostEstimate(flops=flops, bytes_accessed=moved, transcendentals=0),
    )


def shape(dims, kind):
    return jax.ShapeDtypeStruct(dims, kind)


def lanes(dims):
    return lax.broadcasted_iota(jnp.int32, dims, len(dims) - 1)


def moved_by(block, step):
    if step == 0:
        return block
    at = lanes(block.shape) + step
    turned = pltpu.roll(block, (-step) % 128, 1)
    return jnp.where((at >= 0) & (at < 128), turned, 0.0)


def pack_body(
    core_at, side_at, field_far, cot_far, filters_far, out, own_far,
    field, cotangent, filters, own_cot, cells, taps, arrived, sent,
):
    core, side = core_at[0], side_at[0]
    own_taps = filters_far.at[pl.ds(11 * core, 16)]
    pairs = ((field_far, field), (cot_far, cotangent), (own_taps, filters))
    copies = [pltpu.make_async_copy(a, b, arrived.at[n]) for n, (a, b) in enumerate(pairs)]
    for copy in copies:
        copy.start()
    copies[0].wait()
    copies[1].wait()
    for r in range(2):
        for z in range(4):
            at = 128 * (4 * r + z)
            mine = cotangent[:, r, z, :]
            own_cot[:, at : at + 128] = mine
            cells[0, :, at : at + 128] = field[:, r, z, :]
            cells[1, :, at : at + 128] = field[:, r, z, :]
            at = CELLS + 128 * z
            cells[jnp.where(side == r, 0, 1), :, at : at + 128] = mine
    sends = [
        pltpu.make_async_copy(cells.at[c // 8], out.at[c, :, pl.ds(0, TAPS_AT)], sent.at[c])
        for c in range(16)
    ]
    sends.append(pltpu.make_async_copy(own_cot, own_far, sent.at[17]))
    for send in sends:
        send.start()
    copies[2].wait()
    lane = lanes((OWN, 128))
    for g in range(2):
        parts = [jnp.zeros((OWN, 128), F32) for _ in range(16)]
        for j in range(8):
            here = (lane >= 16 * j) & (lane < 16 * j + 16)
            tap = filters[8 * g + j].astype(F32)
            for h in range(2):
                block = tap[:, 128 * h : 128 * h + 128]
                for q in range(8):
                    step = (16 * (j - q)) % 128
                    turned = block if step == 0 else pltpu.roll(block, step, 1)
                    parts[8 * h + q] = jnp.where(here, turned, parts[8 * h + q])
        for c in range(16):
            taps[g, c] = parts[c].astype(BF)
        there = out.at[:, :, pl.ds(TAPS_AT + 128 * g, 128)]
        sends.append(pltpu.make_async_copy(taps.at[g], there, sent.at[18 if g else 16]))
        sends[-1].start()
    for send in sends:
        send.wait()


def taps_sum(products, a, sign):
    blocks = []
    for r in range(2):
        for z in range(4):
            total = None
            for c in range(3):
                column = None
                for b in range(3):
                    source = z + sign * 2 * (b - 1)
                    if source < 0 or source > 3:
                        continue
                    k = 9 * a + 3 * b + c
                    lane = 128 * (4 * r + source)
                    part = products[16 * k : 16 * k + 16, lane : lane + 128]
                    column = part if column is None else column + part
                column = moved_by(column, sign * 2 * (c - 1))
                total = column if total is None else total + column
            blocks.append(total)
    return blocks


def shift_body(below, own, above, shifted):
    zero = jnp.zeros((OWN, 128), BF)
    for a, source in ((0, above), (1, own), (2, below)):
        for r in range(2):
            rolled = []
            for z in range(4):
                lane = 128 * (4 * r + z)
                block = source[:, lane : lane + 128].astype(F32)
                rolled.append([moved_by(block, -2 * (c - 1)).astype(BF) for c in range(3)])
            for z in range(4):
                for b in range(3):
                    at = z - 2 * (b - 1)
                    for c in range(3):
                        k = 9 * a + 3 * b + c
                        lane = 128 * (4 * r + z)
                        shifted[16 * k : 16 * k + 16, lane : lane + 128] = (
                            rolled[at][c] if 0 <= at < 4 else zero
                        )


def grad_body(gathered, shifted, out):
    total = lax.dot_general(
        shifted[...],
        gathered[:, 0:CELLS],
        (((1,), (1,)), ((), ())),
        preferred_element_type=F32,
    )
    power, scaled = scaled_down(total)
    for n in range(8):
        out[n, 0:PART, :] = scaled[PART * n : PART * n + PART, :]
        out[n, PART : PART + 2, :] = jnp.broadcast_to(power, (2, 256))


def parts_body(gathered, _after, cells, taps):
    cells[...] = gathered[:, CELLS:TAPS_AT]
    taps[...] = gathered[:, TAPS_AT:WIDE]


def scaled_down(values):
    most = jnp.full((1, 256), jnp.max(jnp.abs(values)), F32)
    power = jnp.ceil(jnp.log2(jnp.maximum(most, 2.0**-100)))
    return power, values * jnp.exp2(14.0 - power)


def sum_body(factor, peers, parts, *rest):
    out = rest[-1]
    total = jnp.zeros((PART, 256), F32)
    for n in range(peers):
        total = total + parts[n, 0:PART, :] * jnp.exp2(parts[n, PART : PART + 1, :] - 14.0)
    power, scaled = scaled_down(total * factor)
    for n in range(out.shape[0]):
        out[n, 0:PART, :] = scaled
        out[n, PART : PART + 2, :] = jnp.broadcast_to(power, (2, 256))


def finish_body(full, out_far, out, sent):
    half = ROWS // 2
    copies = []
    for h in range(2):
        for n in range(4 * h, 4 * h + 4):
            scale = jnp.exp2(full[n, PART : PART + 1, :] - 14.0)
            out[PART * n : PART * n + PART, :] = full[n, 0:PART, :] * scale
        here = pl.ds(half * h, half)
        copies.append(pltpu.make_async_copy(out.at[here], out_far.at[here], sent.at[h]))
        copies[h].start()
    for copy in copies:
        copy.wait()


def far_body(own, far, out):
    out[...] = own[...] + far[...]


def outputs_body(own, near, out_field, input_grad):
    for out, at in ((out_field, 0), (input_grad, OWN)):
        for r in range(2):
            for z in range(4):
                here = (slice(at, at + OWN), slice(128 * (4 * r + z), 128 * (4 * r + z) + 128))
                out[:, r, z, :] = (own[here] + near[here]).astype(BF)


def contributions_body(core, side_at, gathered, filters, swapped, halves, near, far, mid, products):
    first, side = core[0] == 0, side_at[0]
    products[...] = jnp.dot(
        filters[...].reshape(ROWS, 256), gathered[:, 0:CELLS], preferred_element_type=F32
    )
    put(products, 1, first, 0, near, far, mid)
    mine = gathered[:, TAPS_AT:WIDE]
    other = swapped[...]
    low, high = jnp.where(first, mine, other), jnp.where(first, other, mine)
    over = (((0,), (0,)), ((), ()))
    for r in range(2):
        rows = []
        for line in range(2):
            here = slice(128 * line, 128 * line + 128)
            kept = (side == line) if r == 0 else (side != line)
            rows.append(jnp.where(kept, gathered[here, CELLS:TAPS_AT], halves[here, :]))
        cells = jnp.concatenate(rows, axis=0)
        at = slice(HALF_CELLS * r, HALF_CELLS * r + HALF_CELLS)
        products[0:256, at] = lax.dot_general(low, cells, over, preferred_element_type=F32)
        products[176:ROWS, at] = lax.dot_general(high, cells, over, preferred_element_type=F32)
    put(products, -1, first, OWN, near, far, mid)


def put(products, sign, first, at, near, far, mid):
    following, last = taps_sum(products, 1 - sign, sign), taps_sum(products, 1 + sign, sign)
    for n, block in enumerate(taps_sum(products, 1, sign)):
        here = (slice(at, at + OWN), slice(128 * n, 128 * n + 128))
        mid[here] = block
        near[here] = jnp.where(first, following[n], last[n])
        far[here] = jnp.where(first, last[n], following[n])


def per_device(field, filters, cotangent):
    space = ("far", "near", "core")
    chan = ("side", "line")
    core, side = (lax.axis_index(name).astype(jnp.int32).reshape(1) for name in ("core", "side"))
    up = [(i, i + 1) for i in range(31)]
    down = [(i + 1, i) for i in range(31)]
    swap = [(0, 1), (1, 0)]
    across = [pair for i in range(1, 31, 2) for pair in ((i, i + 1), (i + 1, i))]

    packed, own_cot = call(
        pack_body,
        [shape((16, OWN, WIDE), BF), shape((OWN, CELLS), BF)],
        [SMEM] * 2 + [FAR] * 3,
        [
            pltpu.VMEM((OWN, 2, 4, 128), BF),
            pltpu.VMEM((OWN, 2, 4, 128), BF),
            pltpu.VMEM((16, OWN, 256), BF),
            pltpu.VMEM((OWN, CELLS), BF),
            pltpu.VMEM((2, OWN, TAPS_AT), BF),
            pltpu.VMEM((2, 16, OWN, 128), BF),
            pltpu.SemaphoreType.DMA((3,)),
            pltpu.SemaphoreType.DMA((19,)),
        ],
        moved=1 << 20,
        limit=PACK_LIMIT,
        outs_at=[FAR, FAR],
    )(core, side, field, cotangent, filters)
    gathered = lax.all_to_all(packed, chan, 0, 0).reshape(256, WIDE)
    below = lax.ppermute(own_cot, space, up)
    above = lax.ppermute(own_cot, space, down)

    shifted = call(shift_body, [shape((ROWS, CELLS), BF)], [VMEM] * 3, moved=1 << 20)(
        below, own_cot, above
    )[0]
    own_grad = call(
        grad_body,
        [shape((8, PART + 2, 256), F32)],
        [VMEM] * 2,
        flops=2 * ROWS * CELLS * 256,
        moved=1 << 20,
    )(gathered, shifted)[0]
    half_cells, half_taps = call(
        parts_body, [shape((256, HALF_CELLS), BF), shape((256, 256), BF)], [VMEM, ANY], moved=1 << 19
    )(gathered, own_grad)
    halves = lax.ppermute(half_cells, "side", swap)
    swapped = lax.ppermute(half_taps, "core", swap)
    parts = lax.all_to_all(own_grad.astype(HALF), ("core", "near"), 0, 0).astype(F32)
    to_near, to_far, own_sums = call(
        contributions_body,
        [shape((2 * OWN, CELLS), F32)] * 3,
        [SMEM] * 2 + [VMEM] * 4,
        [pltpu.VMEM((ROWS, CELLS), F32)],
        flops=CONTRIBUTIONS_FLOPS,
        moved=1 << 20,
    )(core, side, gathered, filters, swapped, halves)
    from_far = lax.ppermute(to_far, space, across)

    def summed(factor, peers, following, flops, parts, *after):
        body = functools.partial(sum_body, factor, peers)
        outs = [shape((following, PART + 2, 256), F32)]
        return call(body, outs, [VMEM] + [ANY] * len(after), flops=flops)(parts, *after)[0]

    def spread(many, axes):
        return lax.all_to_all(many.astype(HALF), axes, 0, 0).astype(F32)

    row = summed(1.0, 8, 4, ROW_FLOPS, parts)
    mine = summed(SCALE, 4, 8, 0, spread(row, "far"), own_sums)
    from_near = lax.ppermute(to_near, "core", swap)
    full = spread(mine, ("core", "near"))
    weight_grad = call(
        finish_body,
        [shape((ROWS, 256), F32)],
        [VMEM],
        [pltpu.VMEM((ROWS, 256), F32), pltpu.SemaphoreType.DMA((2,))],
        moved=1 << 20,
        outs_at=[FAR],
    )(full)[0]
    own_and_far = call(far_body, [shape((2 * OWN, CELLS), F32)], [VMEM] * 2, flops=FAR_FLOPS)(
        own_sums, from_far
    )[0]
    out_field, input_grad = call(outputs_body, [shape(field.shape, BF)] * 2, [VMEM] * 2, moved=1 << 18)(
        own_and_far, from_near
    )
    return out_field, input_grad, weight_grad.reshape(TAPS, OWN, 256)


def solution(mesh):
    fine = Mesh(mesh.devices.reshape(4, 4, 2, 2, 8), ("far", "near", "core", "side", "line"))
    cells = P(("side", "line"), ("far", "near", "core"), None, None)
    taps = P(None, ("side", "line"), None)
    return jax.shard_map(
        per_device,
        mesh=fine,
        in_specs=(cells, taps, cells),
        out_specs=(cells, cells, taps),
        check_vma=False,
    )
```
